256 devices in a mesh: dp: 4 (over y), ctx: 64 (over z, x, core).
Axes of the slice: x: 4, y: 4, z: 8, core: 2. Of those that a mesh axis runs over, the one named last changes fastest.
Arguments:
- out_grad: float32 [4, 16, 131072], P('dp', None, 'ctx'), may hold values from -6 to 6
- conv_input: float32 [4, 16, 131072], P('dp', None, 'ctx'), may hold values from -0.001953125 to 0.001953125
- filter_taps: float32 [131072], P('ctx'), may hold values from -0.015625 to 0.015625
- skip_gain: float32 [16], replicated, may hold values from 0.5 to 2
Outputs:
- input_grad: float32 [4, 16, 131072], P('dp', None, 'ctx')
- filter_grad: float32 [131072], P('ctx')
The draws below stay inside these ranges and needn't reach their ends.
All inputs are finite; a program needn't handle non-finite values.
Results may differ from the reference program's by a relative error of at most 0.00012.
Values sent between devices are 32-bit elements; how exact they have to be, the bound alone decides.
No kernel may reach another device: no remote copies, remote signals or barrier semaphores. Data moves between devices by JAX's collectives and lax.ppermute only.
A program may use at most 64 MiB of HBM per device.

```python
import jax
import jax.numpy as jnp
from jax import lax

CH = 16
SEQ = 131072
BATCH = 4


def block_levels(stream_key, shape, split, least, largest):
    gain, own = 1.0, jax.random.fold_in(stream_key, 6)
    for dim, blocks in split:
        draws = jnp.exp(jax.random.uniform(jax.random.fold_in(own, dim), (blocks,), jnp.float32, least / len(split), largest / len(split)))
        gain = gain * jnp.repeat(draws, shape[dim] // blocks).reshape([-1 if axis == dim else 1 for axis in range(len(shape))])
    return gain


def noise(rng, dims, scale, limit, split=(), kind=jnp.bfloat16):
    drawn = scale * jax.random.normal(rng, dims, jnp.float32)
    if split:
        drawn = drawn * block_levels(rng, dims, split, -0.22, 0.18)
    return jnp.clip(drawn, -limit, limit).astype(kind)


def setup_inputs(seed: int = 0) -> dict:
    arg_keys = jax.random.split(jax.random.key(seed), 5)
    return {
        "out_grad": noise(arg_keys[0], (BATCH, CH, SEQ), 1.0, 6.0, ((0, 4), (2, 64)), jnp.float32),
        "conv_input": noise(arg_keys[1], (BATCH, CH, SEQ), (BATCH * CH * SEQ) ** -0.5, 0.001953125, ((0, 4), (2, 64)), jnp.float32),
        "filter_taps": noise(arg_keys[2], (SEQ,), SEQ ** -0.5, 0.015625, ((0, 64),), jnp.float32),
        "skip_gain": jnp.clip(jax.random.uniform(arg_keys[3], (CH,), jnp.float32, 0.5, 2.0), 0.5, 2.0),
    }


def reference(out_grad, conv_input, filter_taps, skip_gain):
    fft_len = 2 * SEQ
    filter_spec = jnp.fft.rfft(filter_taps, n=fft_len, axis=-1)

    def per_group(pair):
        grad_rows, input_rows = pair
        grad_spec = jnp.fft.rfft(grad_rows, n=fft_len, axis=-1)
        input_spec = jnp.fft.rfft(input_rows, n=fft_len, axis=-1)
        dx_full = jnp.fft.irfft(jnp.conj(filter_spec)[None, :] * grad_spec, n=fft_len, axis=-1)[:, :SEQ]
        dh_full = jnp.fft.irfft(grad_spec * jnp.conj(input_spec), n=fft_len, axis=-1)[:, :SEQ]
        return dx_full + skip_gain[:, None] * grad_rows, jnp.sum(dh_full, axis=0)

    input_grad, filter_parts = lax.map(per_group, (out_grad, conv_input))
    return input_grad, jnp.sum(filter_parts, axis=0)
```

```python
import functools

import jax
import jax.numpy as jnp
import ml_dtypes
import numpy as np
from jax import lax
from jax.experimental import pallas as pl
from jax.experimental.pallas import tpu as pltpu
from jax.sharding import Mesh, PartitionSpec as P

Y, Z, X, C = 4, 8, 4, 2
ROWS_IN, ROWS_OUT = 5, 3
SUB, LANES = 16, 128
POINTS = 128
SCALE = 1.0 / 131072.0


def class_of(x, c):
    return 2 * x + c


def z_tables():
    out = np.zeros((X * C, 2, X, 2, Z))
    z = np.arange(Z)
    for x in range(X):
        for c in range(C):
            for other in range(2):
                for shift in range(X):
                    k = class_of((x + shift) % X, c ^ other) + 0.5
                    angle = 2.0 * np.pi * z * k / 16.0
                    out[class_of(x, c), other, shift, 0] = np.cos(angle)
                    out[class_of(x, c), other, shift, 1] = -np.sin(angle)
    return out.reshape(X * C, -1).astype(np.float32)


def numpy_split(table):
    table = table.astype(np.float32)
    high = table.astype(ml_dtypes.bfloat16)
    low = (table - high.astype(np.float32)).astype(ml_dtypes.bfloat16)
    return high, low


def left_tables():
    out = np.zeros((X * C, 2, POINTS, X, C, 2, SUB))
    alpha = np.arange(POINTS)[:, None]
    for x in range(X):
        for c in range(C):
            k = class_of(x, c) + 0.5
            for shift in range(X):
                for other in range(C):
                    p = class_of((x - shift) % X, c ^ other)
                    a = p * SUB + np.arange(SUB)[None, :]
                    angle = -2.0 * np.pi * ((a * alpha % POINTS) / POINTS + a * k / 2048.0)
                    at = out[class_of(x, c), :, :, shift, other]
                    at[0, :, 0], at[0, :, 1] = np.cos(angle), -np.sin(angle)
                    at[1, :, 0], at[1, :, 1] = np.sin(angle), np.cos(angle)
    return out.reshape(X * C, 2 * POINTS, 2 * POINTS)


def twiddle_tables():
    out = np.zeros((X * C, 2, POINTS, LANES))
    alpha, b = np.arange(POINTS)[:, None], np.arange(LANES)[None, :]
    for p in range(X * C):
        angle = -2.0 * np.pi * b * (alpha + (p + 0.5) / 16.0) / 16384.0
        out[p, 0], out[p, 1] = np.cos(angle), np.sin(angle)
    return out.astype(np.float32)


def right_table():
    b = np.arange(LANES)
    angle = -2.0 * np.pi * (b[:, None] * b[None, :] % LANES) / LANES
    cosine, sine = np.cos(angle), np.sin(angle)
    return np.block([[cosine, sine], [-sine, cosine]])


def z_forward_kernel(coef_ref, in_ref, keep_ref, send_ref):
    for row in range(ROWS_IN):
        blocks = [in_ref[z, row] for z in range(Z)]
        for half, out_ref in enumerate((keep_ref, send_ref)):
            for shift in range(X):
                for part in range(2):
                    base = ((half * X + shift) * 2 + part) * Z
                    total = coef_ref[base] * blocks[0]
                    for z in range(1, Z):
                        total = total + coef_ref[base + z] * blocks[z]
                    out_ref[shift, row, part] = total


def z_inverse_kernel(coef_ref, own_ref, other_ref, out_ref):
    for row in range(ROWS_OUT):
        totals = [None] * Z
        for half, in_ref in enumerate((own_ref, other_ref)):
            for shift in range(X):
                for part in range(2):
                    base = ((half * X + shift) * 2 + part) * Z
                    value = in_ref[shift, row, part]
                    for z in range(Z):
                        term = coef_ref[base + z] * value
                        totals[z] = term if totals[z] is None else totals[z] + term
        for z in range(Z):
            out_ref[z, row] = totals[z] * SCALE


def split(value):
    high = value.astype(jnp.bfloat16)
    return high, (value - high.astype(jnp.float32)).astype(jnp.bfloat16)


def product(left, right):
    (left_high, left_low), (right_high, right_low) = left, right
    dot = functools.partial(jnp.dot, preferred_element_type=jnp.float32)
    return dot(left_high, right_high) + (dot(left_high, right_low) + dot(left_low, right_high))


def spectral_kernel(
    x0, x1, x2, x3, wh, wl, wth, wtl, tw, bh, bl, bth, btl, o0, o1, o2, o3
):
    chunks, outs = (x0, x1, x2, x3), (o0, o1, o2, o3)
    pieces = [(s, c, part) for s in range(X) for c in range(C) for part in range(2)]
    columns = [
        jnp.concatenate([chunks[s][c, row, part] for s, c, part in pieces], axis=0)
        for row in range(ROWS_IN)
    ]
    value = product((wh[...], wl[...]), split(jnp.concatenate(columns, axis=1)))
    cosine, sine = tw[0], tw[1]
    rows = []
    for row in range(ROWS_IN):
        lanes = slice(row * LANES, (row + 1) * LANES)
        real, imag = value[:POINTS, lanes], value[POINTS:, lanes]
        rows.append(
            jnp.concatenate([real * cosine - imag * sine, real * sine + imag * cosine], axis=1)
        )
    value = product(split(jnp.concatenate(rows, axis=0)), (bh[...], bl[...]))
    real = [value[row * POINTS : (row + 1) * POINTS, :LANES] for row in range(ROWS_IN)]
    imag = [value[row * POINTS : (row + 1) * POINTS, LANES:] for row in range(ROWS_IN)]
    rows = []
    for channel in range(2):
        gr, gi = real[channel], imag[channel]
        rows.append(
            jnp.concatenate([real[4] * gr + imag[4] * gi, real[4] * gi - imag[4] * gr], axis=1)
        )
    dh_real, dh_imag = 0.0, 0.0
    for channel in range(2):
        gr, gi, ur, ui = real[channel], imag[channel], real[2 + channel], imag[2 + channel]
        dh_real = dh_real + (gr * ur + gi * ui)
        dh_imag = dh_imag + (gi * ur - gr * ui)
    rows.append(jnp.concatenate([dh_real, dh_imag], axis=1))
    value = product(split(jnp.concatenate(rows, axis=0)), (bth[...], btl[...]))
    columns = []
    for row in range(ROWS_OUT):
        vr = value[row * POINTS : (row + 1) * POINTS, :LANES]
        vi = value[row * POINTS : (row + 1) * POINTS, LANES:]
        columns.append(
            jnp.concatenate([vr * cosine + vi * sine, vi * cosine - vr * sine], axis=0)
        )
    value = product((wth[...], wtl[...]), split(jnp.concatenate(columns, axis=1)))
    for index, (s, c, part) in enumerate(pieces):
        for row in range(ROWS_OUT):
            outs[s][c, row, part] = value[
                index * SUB : (index + 1) * SUB, row * LANES : (row + 1) * LANES
            ]


VMEM = pl.BlockSpec(memory_space=pltpu.VMEM)
SMEM = pl.BlockSpec(memory_space=pltpu.SMEM)
PARAMS = pltpu.CompilerParams(vmem_limit_bytes=32 * 1024 * 1024)


def f32(*shape):
    return jax.ShapeDtypeStruct(shape, jnp.float32)


def shift_x(value, shift):
    return lax.ppermute(value, "x", [(i, (i + shift) % X) for i in range(X)])


def swap_core(value):
    return lax.ppermute(value, "c", [(0, 1), (1, 0)])


def pair_y(value, partner):
    return lax.ppermute(value, "y", [(i, partner(i)) for i in range(Y)])


def per_device(out_grad, conv_input, filter_taps, skip_gain):
    place = class_of(lax.axis_index("x"), lax.axis_index("c"))

    def mine(table):
        return lax.dynamic_index_in_dim(jnp.asarray(table), place, 0, keepdims=False)

    coef = mine(z_tables())
    left = left_tables()
    wh, wl = (mine(t) for t in numpy_split(left))
    wth, wtl = (mine(t) for t in numpy_split(np.swapaxes(left, 1, 2)))
    twiddle = mine(twiddle_tables())
    right = right_table()
    bh, bl = (jnp.asarray(t) for t in numpy_split(right))
    bth, btl = (jnp.asarray(t) for t in numpy_split(right.T))

    blocks = jnp.concatenate(
        [
            out_grad.reshape(Z, 2, SUB, LANES),
            conv_input.reshape(Z, 2, SUB, LANES),
            jnp.broadcast_to(filter_taps.reshape(1, 1, SUB, LANES), (Z, 1, SUB, LANES)),
        ],
        axis=1,
    )
    blocks = lax.all_to_all(blocks, "z", 0, 0, tiled=True)
    tile = (SUB, LANES)
    kept, sent = pl.pallas_call(
        z_forward_kernel,
        out_shape=[f32(X, ROWS_IN, 2, *tile)] * 2,
        in_specs=[SMEM, VMEM],
        out_specs=[VMEM] * 2,
        compiler_params=PARAMS,
    )(coef, blocks)
    crossed = swap_core(sent)
    chunks = [jnp.stack([kept[s], crossed[s]]) for s in range(X)]
    chunks = [chunks[0]] + [shift_x(chunks[s], s) for s in range(1, X)]
    chunks = pl.pallas_call(
        spectral_kernel,
        out_shape=[f32(C, ROWS_OUT, 2, *tile)] * X,
        in_specs=[VMEM] * 13,
        out_specs=[VMEM] * X,
        compiler_params=PARAMS,
    )(*chunks, wh, wl, wth, wtl, twiddle, bh, bl, bth, btl)
    chunks = [chunks[0]] + [shift_x(chunks[s], -s) for s in range(1, X)]
    own = jnp.stack([chunk[0] for chunk in chunks])
    other = swap_core(jnp.stack([chunk[1] for chunk in chunks]))
    blocks = pl.pallas_call(
        z_inverse_kernel,
        out_shape=f32(Z, ROWS_OUT, *tile),
        in_specs=[SMEM, VMEM, VMEM],
        out_specs=VMEM,
        compiler_params=PARAMS,
    )(coef, own, other)
    blocks = lax.all_to_all(blocks, "z", 0, 0, tiled=True)
    filter_grad = jnp.sum(blocks[:, 2], axis=0)
    near = pair_y(filter_grad, lambda i: i ^ 1)
    far = pair_y(filter_grad, lambda i: Y - 1 - i)
    across = pair_y(filter_grad, lambda i: i ^ 2)
    filter_grad = (filter_grad + near) + (far + across)
    input_grad = blocks[:, :2].reshape(out_grad.shape) + skip_gain[None, :, None] * out_grad
    return (input_grad, filter_grad.reshape(filter_taps.shape))


def solution(mesh):
    fine = Mesh(mesh.devices.reshape(Y, Z, X, C), ("y", "z", "x", "c"))
    return jax.shard_map(
        per_device,
        mesh=fine,
        in_specs=(P("y", None, ("z", "x", "c")), P("y", None, ("z", "x", "c")), P(("z", "x", "c")), P()),
        out_specs=(P("y", None, ("z", "x", "c")), P(("z", "x", "c"))),
        check_vma=False,
    )
```

```python
import functools
import math

import jax
import jax.numpy as jnp
import ml_dtypes
import numpy as np
from jax import lax
from jax.experimental import pallas as pl
from jax.experimental.pallas import tpu as pltpu
from jax.sharding import Mesh, PartitionSpec as P

Y, Z, X, C = 4, 8, 4, 2
ROWS_IN, ROWS_OUT = 5, 3
ORDER_IN, ORDER_OUT = (2, 0, 1, 3), (0, 2, 1, 3)
SUB, LANES = 16, 128
POINTS = 128
SCALE = 1.0 / 131072.0


def class_of(x, c):
    return 2 * x + c


def z_weight(x, parity, part, z):
    def weight(k):
        angle = math.pi * (2 * k + 1) * z / 16.0
        return math.cos(angle) if part == 0 else -math.sin(angle)

    return jnp.where(parity == 0, jnp.float32(weight(2 * x)), jnp.float32(weight(2 * x + 1)))


def slot_of(x, place, order):
    shift = (x - place // 2) & (X - 1)
    slot = jnp.int32(order.index(0))
    for other in range(1, X):
        slot = jnp.where(shift == other, order.index(other), slot)
    return slot


def numpy_split(table):
    table = table.astype(np.float32)
    high = table.astype(ml_dtypes.bfloat16)
    low = (table - high.astype(np.float32)).astype(ml_dtypes.bfloat16)
    return high, low


def left_tables(order):
    out = np.zeros((X * C, 2, POINTS, X, C, 2, SUB))
    alpha = np.arange(POINTS)[:, None]
    for x in range(X):
        for c in range(C):
            k = class_of(x, c) + 0.5
            for slot, shift in enumerate(order):
                for other in range(C):
                    p = class_of((x - shift) % X, c ^ other)
                    a = p * SUB + np.arange(SUB)[None, :]
                    angle = -2.0 * np.pi * ((a * alpha % POINTS) / POINTS + a * k / 2048.0)
                    at = out[class_of(x, c), :, :, slot, other]
                    at[0, :, 0], at[0, :, 1] = np.cos(angle), -np.sin(angle)
                    at[1, :, 0], at[1, :, 1] = np.sin(angle), np.cos(angle)
    return out.reshape(X * C, 2 * POINTS, 2 * POINTS)


def twiddle_tables():
    out = np.zeros((X * C, 2, POINTS, LANES))
    alpha, b = np.arange(POINTS)[:, None], np.arange(LANES)[None, :]
    for p in range(X * C):
        angle = -2.0 * np.pi * b * (alpha + (p + 0.5) / 16.0) / 16384.0
        out[p, 0], out[p, 1] = np.cos(angle), np.sin(angle)
    return out.astype(np.float32)


def right_table():
    b = np.arange(LANES)
    angle = -2.0 * np.pi * (b[:, None] * b[None, :] % LANES) / LANES
    cosine, sine = np.cos(angle), np.sin(angle)
    return np.block([[cosine, sine], [-sine, cosine]])


def pack_kernel(place_ref, grad_hbm, input_hbm, filter_hbm, out_ref, grad_ref, input_ref, filter_ref, sems):
    pairs = ((grad_hbm.at[0], grad_ref), (input_hbm.at[0], input_ref), (filter_hbm, filter_ref))
    copies = [pltpu.make_async_copy(*pair, sems.at[i]) for i, pair in enumerate(pairs)]
    for copy in copies:
        copy.start()
    for first, ref in ((0, grad_ref), (2, input_ref)):
        copies[first // 2].wait()
        values = ref[...].reshape(Z * 2, SUB, LANES)
        for z in range(Z):
            for row in range(2):
                out_ref[z, first + row] = values[2 * z + row]
    copies[2].wait()
    for z in range(Z):
        out_ref[z, 4] = filter_ref[...]


def z_forward_kernel(half, place_ref, in_ref, *out_refs):
    place = place_ref[0]
    parity = (place & 1) ^ half
    for x in range(X):
        slot = slot_of(x, place, ORDER_IN)
        for part in range(2):
            total = None
            for z in range(Z):
                term = z_weight(x, parity, part, z) * in_ref[z]
                total = term if total is None else total + term
            out_refs[0][slot, :, part] = total


def z_inverse_sums(half, place_ref, in_ref):
    place = place_ref[0]
    parity = (place & 1) ^ half
    slots = [slot_of(x, place, ORDER_OUT) for x in range(X)]
    values = [[in_ref[slots[x], :, part] for part in range(2)] for x in range(X)]
    for z in range(Z):
        total = None
        for x in range(X):
            for part in range(2):
                term = (z_weight(x, parity, part, z) * SCALE) * values[x][part]
                total = term if total is None else total + term
        yield z, total


def z_inverse_own_kernel(place_ref, skip_ref, in_ref, packed_ref, out_ref, skipped_ref):
    for z, total in z_inverse_sums(0, place_ref, in_ref):
        out_ref[z] = total
    for channel in range(Z * 2):
        z, row = divmod(channel, 2)
        skipped_ref[z, row] = skip_ref[channel] * packed_ref[z, row]


def z_inverse_other_kernel(place_ref, in_ref, own_ref, out_ref):
    for z, total in z_inverse_sums(1, place_ref, in_ref):
        out_ref[z] = own_ref[z] + total


def split(value):
    high = value.astype(jnp.bfloat16)
    return high, (value - high.astype(jnp.float32)).astype(jnp.bfloat16)


def product(left, right):
    (left_high, left_low), (right_high, right_low) = left, right
    dot = functools.partial(jnp.dot, preferred_element_type=jnp.float32)
    return dot(left_high, right_high) + (dot(left_high, right_low) + dot(left_low, right_high))


def spectral_kernel(
    x0, x1, x2, x3, left, tw, right, o0, o1, o2, o3
):
    chunks, outs = (x0, x1, x2, x3), (o0, o1, o2, o3)
    wh, wl, wth, wtl = (left[i] for i in range(4))
    bh, bl, bth, btl = (right[i] for i in range(4))
    pieces = [(s, c, part) for s in range(X) for c in range(C) for part in range(2)]
    columns = [
        jnp.concatenate([chunks[s][c, row, part] for s, c, part in pieces], axis=0)
        for row in range(ROWS_IN)
    ]
    value = product((wh, wl), split(jnp.concatenate(columns, axis=1)))
    cosine, sine = tw[0], tw[1]
    rows = []
    for row in range(ROWS_IN):
        lanes = slice(row * LANES, (row + 1) * LANES)
        real, imag = value[:POINTS, lanes], value[POINTS:, lanes]
        rows.append(
            jnp.concatenate([real * cosine - imag * sine, real * sine + imag * cosine], axis=1)
        )
    value = product(split(jnp.concatenate(rows, axis=0)), (bh, bl))
    real = [value[row * POINTS : (row + 1) * POINTS, :LANES] for row in range(ROWS_IN)]
    imag = [value[row * POINTS : (row + 1) * POINTS, LANES:] for row in range(ROWS_IN)]
    rows = []
    for channel in range(2):
        gr, gi = real[channel], imag[channel]
        rows.append(
            jnp.concatenate([real[4] * gr + imag[4] * gi, real[4] * gi - imag[4] * gr], axis=1)
        )
    dh_real, dh_imag = 0.0, 0.0
    for channel in range(2):
        gr, gi, ur, ui = real[channel], imag[channel], real[2 + channel], imag[2 + channel]
        dh_real = dh_real + (gr * ur + gi * ui)
        dh_imag = dh_imag + (gi * ur - gr * ui)
    rows.append(jnp.concatenate([dh_real, dh_imag], axis=1))
    value = product(split(jnp.concatenate(rows, axis=0)), (bth, btl))
    columns = []
    for row in range(ROWS_OUT):
        vr = value[row * POINTS : (row + 1) * POINTS, :LANES]
        vi = value[row * POINTS : (row + 1) * POINTS, LANES:]
        columns.append(
            jnp.concatenate([vr * cosine + vi * sine, vi * cosine - vr * sine], axis=0)
        )
    value = product((wth, wtl), split(jnp.concatenate(columns, axis=1)))
    for index, (s, c, part) in enumerate(pieces):
        for row in range(ROWS_OUT):
            outs[s][c, row, part] = value[
                index * SUB : (index + 1) * SUB, row * LANES : (row + 1) * LANES
            ]


VMEM = pl.BlockSpec(memory_space=pltpu.VMEM)
HBM = pl.BlockSpec(memory_space=pltpu.HBM)
SMEM = pl.BlockSpec(memory_space=pltpu.SMEM)
PARAMS = pltpu.CompilerParams(vmem_limit_bytes=32 * 1024 * 1024)


def f32(*shape):
    return jax.ShapeDtypeStruct(shape, jnp.float32)


def shift_x(value, shift):
    return lax.ppermute(value, "x", [(i, (i + shift) % X) for i in range(X)])


def swap_core(value):
    return lax.ppermute(value, "c", [(0, 1), (1, 0)])


def pair_y(value, partner):
    return lax.ppermute(value, "y", [(i, partner(i)) for i in range(Y)])


def per_device(out_grad, conv_input, filter_taps, skip_gain):
    place = class_of(lax.axis_index("x"), lax.axis_index("c"))

    def mine(table):
        return lax.dynamic_index_in_dim(jnp.asarray(table), place, 0, keepdims=False)

    tile = (SUB, LANES)
    scalar = place.reshape(1)
    matrix = right_table()
    right = jnp.asarray(np.stack(numpy_split(matrix) + numpy_split(matrix.T)))

    packed = pl.pallas_call(
        pack_kernel,
        out_shape=f32(Z, ROWS_IN, *tile),
        in_specs=[SMEM] + [HBM] * 3,
        out_specs=VMEM,
        scratch_shapes=[
            pltpu.VMEM((Z * 2, SUB * LANES), jnp.float32),
            pltpu.VMEM((Z * 2, SUB * LANES), jnp.float32),
            pltpu.VMEM(tile, jnp.float32),
            pltpu.SemaphoreType.DMA((3,)),
        ],
        compiler_params=pltpu.CompilerParams(vmem_limit_bytes=60 * 1024 * 1024),
    )(scalar, out_grad, conv_input, filter_taps.reshape(tile))
    blocks = lax.all_to_all(packed, "z", 0, 0, tiled=True)

    def z_forward(half):
        return pl.pallas_call(
            functools.partial(z_forward_kernel, half),
            out_shape=f32(X, ROWS_IN, 2, *tile),
            in_specs=[SMEM, VMEM],
            out_specs=VMEM,
            compiler_params=PARAMS,
        )(scalar, blocks)

    sent = z_forward(1)
    first = swap_core(sent[0])
    crossed = swap_core(sent[1:])
    kept = z_forward(0)
    chunks = [jnp.stack([kept[0], first])] + [jnp.stack([kept[i], crossed[i - 1]]) for i in range(1, X)]
    place, chunks[0] = lax.optimization_barrier((place, chunks[0]))
    matrix, back = left_tables(ORDER_IN), np.swapaxes(left_tables(ORDER_OUT), 1, 2)
    left = mine(np.stack(numpy_split(matrix) + numpy_split(back), axis=1))
    twiddle = mine(twiddle_tables())
    chunks = [shift_x(chunk, s) if s else chunk for chunk, s in zip(chunks, ORDER_IN)]
    chunks = pl.pallas_call(
        spectral_kernel,
        out_shape=[f32(C, ROWS_OUT, 2, *tile)] * X,
        in_specs=[VMEM] * 7,
        out_specs=[VMEM] * X,
        compiler_params=PARAMS,
    )(*chunks, left, twiddle, right)
    chunks = [shift_x(chunk, -s) if s else chunk for chunk, s in zip(chunks, ORDER_OUT)]
    own = jnp.stack([chunk[0] for chunk in chunks])
    other = swap_core(jnp.stack([chunk[1] for chunk in chunks]))

    partial, skipped = pl.pallas_call(
        z_inverse_own_kernel,
        out_shape=[f32(Z, ROWS_OUT, *tile), f32(Z, 2, *tile)],
        in_specs=[SMEM, SMEM, VMEM, VMEM],
        out_specs=[VMEM] * 2,
        compiler_params=PARAMS,
    )(scalar, skip_gain, own, packed)
    blocks = pl.pallas_call(
        z_inverse_other_kernel,
        out_shape=f32(Z, ROWS_OUT, *tile),
        in_specs=[SMEM, VMEM, VMEM],
        out_specs=VMEM,
        compiler_params=PARAMS,
    )(scalar, other, partial)
    blocks = lax.all_to_all(blocks, "z", 0, 0, tiled=True)
    filter_grad = jnp.sum(blocks[:, 2], axis=0)
    across = pair_y(filter_grad, lambda i: i ^ 2)
    far = pair_y(filter_grad, lambda i: Y - 1 - i)
    near = pair_y(filter_grad, lambda i: i ^ 1)
    filter_grad = (filter_grad + near) + (far + across)
    input_grad = blocks[:, :2] + skipped
    return (input_grad.reshape(out_grad.shape), filter_grad.reshape(filter_taps.shape))


def solution(mesh):
    fine = Mesh(mesh.devices.reshape(Y, Z, X, C), ("y", "z", "x", "c"))
    return jax.shard_map(
        per_device,
        mesh=fine,
        in_specs=(P("y", None, ("z", "x", "c")), P("y", None, ("z", "x", "c")), P(("z", "x", "c")), P()),
        out_specs=(P("y", None, ("z", "x", "c")), P(("z", "x", "c"))),
        check_vma=False,
    )
```

```python
import functools
import math

import jax
import jax.numpy as jnp
import ml_dtypes
import numpy as np
from jax import lax
from jax.experimental import pallas as pl
from jax.experimental.pallas import tpu as pltpu
from jax.sharding import Mesh, PartitionSpec as P

Y, Z, X, C = 4, 8, 4, 2
ROWS_IN, ROWS_OUT = 5, 3
ORDER_IN, ORDER_OUT = (2, 0, 1, 3), (0, 2, 1, 3)
SUB, LANES = 16, 128
POINTS = 128
SCALE = 1.0 / 131072.0


def class_of(x, c):
    return 2 * x + c


def z_weight(x, parity, part, z):
    def weight(k):
        angle = math.pi * (2 * k + 1) * z / 16.0
        return math.cos(angle) if part == 0 else -math.sin(angle)

    return jnp.where(parity == 0, jnp.float32(weight(2 * x)), jnp.float32(weight(2 * x + 1)))


def slot_of(x, place, order):
    shift = (x - place // 2) & (X - 1)
    slot = jnp.int32(order.index(0))
    for other in range(1, X):
        slot = jnp.where(shift == other, order.index(other), slot)
    return slot


def numpy_split(table):
    table = table.astype(np.float32)
    high = table.astype(ml_dtypes.bfloat16)
    low = (table - high.astype(np.float32)).astype(ml_dtypes.bfloat16)
    return high, low


def left_tables(order):
    out = np.zeros((X * C, 2, POINTS, X, C, 2, SUB))
    alpha = np.arange(POINTS)[:, None]
    for x in range(X):
        for c in range(C):
            k = class_of(x, c) + 0.5
            for slot, shift in enumerate(order):
                for other in range(C):
                    p = class_of((x - shift) % X, c ^ other)
                    a = p * SUB + np.arange(SUB)[None, :]
                    angle = -2.0 * np.pi * ((a * alpha % POINTS) / POINTS + a * k / 2048.0)
                    at = out[class_of(x, c), :, :, slot, other]
                    at[0, :, 0], at[0, :, 1] = np.cos(angle), -np.sin(angle)
                    at[1, :, 0], at[1, :, 1] = np.sin(angle), np.cos(angle)
    return out.reshape(X * C, 2 * POINTS, 2 * POINTS)


def twiddle_tables():
    out = np.zeros((X * C, 2, POINTS, LANES))
    alpha, b = np.arange(POINTS)[:, None], np.arange(LANES)[None, :]
    for p in range(X * C):
        angle = -2.0 * np.pi * b * (alpha + (p + 0.5) / 16.0) / 16384.0
        out[p, 0], out[p, 1] = np.cos(angle), np.sin(angle)
    return out.astype(np.float32)


def right_table():
    b = np.arange(LANES)
    angle = -2.0 * np.pi * (b[:, None] * b[None, :] % LANES) / LANES
    cosine, sine = np.cos(angle), np.sin(angle)
    return np.block([[cosine, sine], [-sine, cosine]])


def pack_kernel(place_ref, grad_hbm, input_hbm, filter_hbm, out_ref, grad_ref, input_ref, filter_ref, sems):
    pairs = ((grad_hbm.at[0], grad_ref), (input_hbm.at[0], input_ref), (filter_hbm, filter_ref))
    copies = [pltpu.make_async_copy(*pair, sems.at[i]) for i, pair in enumerate(pairs)]
    for copy in copies:
        copy.start()
    for first, ref in ((0, grad_ref), (2, input_ref)):
        copies[first // 2].wait()
        values = ref[...].reshape(Z * 2, SUB, LANES)
        for z in range(Z):
            for row in range(2):
                out_ref[z, first + row] = values[2 * z + row]
    copies[2].wait()
    for z in range(Z):
        out_ref[z, 4] = filter_ref[...]


def z_forward_kernel(half, place_ref, in_ref, *out_refs):
    place = place_ref[0]
    parity = (place & 1) ^ half
    for x in range(X):
        slot = slot_of(x, place, ORDER_IN)
        for part in range(2):
            total = None
            for z in range(Z):
                term = z_weight(x, parity, part, z) * in_ref[z]
                total = term if total is None else total + term
            out_refs[0][slot, :, part] = total


def z_inverse_sums(half, place_ref, in_ref):
    place = place_ref[0]
    parity = (place & 1) ^ half
    slots = [slot_of(x, place, ORDER_OUT) for x in range(X)]
    values = [[in_ref[slots[x], :, part] for part in range(2)] for x in range(X)]
    for z in range(Z):
        total = None
        for x in range(X):
            for part in range(2):
                term = (z_weight(x, parity, part, z) * SCALE) * values[x][part]
                total = term if total is None else total + term
        yield z, total


def z_inverse_own_kernel(place_ref, skip_ref, in_ref, packed_ref, out_ref, skipped_ref):
    for z, total in z_inverse_sums(0, place_ref, in_ref):
        out_ref[z] = total
    for channel in range(Z * 2):
        z, row = divmod(channel, 2)
        skipped_ref[z, row] = skip_ref[channel] * packed_ref[z, row]


def z_inverse_other_kernel(place_ref, in_ref, own_ref, out_ref):
    for z, total in z_inverse_sums(1, place_ref, in_ref):
        out_ref[z] = own_ref[z] + total


def split(value):
    high = value.astype(jnp.bfloat16)
    return high, (value - high.astype(jnp.float32)).astype(jnp.bfloat16)


def product(left, right):
    (left_high, left_low), (right_high, right_low) = left, right
    dot = functools.partial(jnp.dot, preferred_element_type=jnp.float32)
    return dot(left_high, right_high) + (dot(left_high, right_low) + dot(left_low, right_high))


def spectral_kernel(
    x0, x1, x2, x3, left, tw, right, o0, o1, o2, o3
):
    chunks, outs = (x0, x1, x2, x3), (o0, o1, o2, o3)
    wh, wl, wth, wtl = (left[i] for i in range(4))
    bh, bl, bth, btl = (right[i] for i in range(4))
    pieces = [(s, c, part) for s in range(X) for c in range(C) for part in range(2)]
    cosine, sine = tw[0], tw[1]

    def forward(*picked):
        columns = [
            jnp.concatenate([chunks[s][c, row, part] for s, c, part in pieces], axis=0)
            for row in picked
        ]
        value = product((wh, wl), split(jnp.concatenate(columns, axis=1)))
        rows = []
        for i in range(len(picked)):
            lanes = slice(i * LANES, (i + 1) * LANES)
            real, imag = value[:POINTS, lanes], value[POINTS:, lanes]
            rows.append(
                jnp.concatenate([real * cosine - imag * sine, real * sine + imag * cosine], axis=1)
            )
        value = product(split(jnp.concatenate(rows, axis=0)), (bh, bl))
        spans = [slice(i * POINTS, (i + 1) * POINTS) for i in range(len(picked))]
        return [(value[span, :LANES], value[span, LANES:]) for span in spans]

    def inverse(spectra, picked):
        rows = jnp.concatenate([jnp.concatenate(pair, axis=1) for pair in spectra], axis=0)
        value = product(split(rows), (bth, btl))
        columns = []
        for i in range(len(picked)):
            span = slice(i * POINTS, (i + 1) * POINTS)
            vr, vi = value[span, :LANES], value[span, LANES:]
            columns.append(
                jnp.concatenate([vr * cosine + vi * sine, vi * cosine - vr * sine], axis=0)
            )
        value = product((wth, wtl), split(jnp.concatenate(columns, axis=1)))
        for index, (s, c, part) in enumerate(pieces):
            for i, row in enumerate(picked):
                outs[s][c, row, part] = value[
                    index * SUB : (index + 1) * SUB, i * LANES : (i + 1) * LANES
                ]

    ((fr, fi),) = forward(4)
    pairs = [forward(channel, 2 + channel) for channel in range(2)]
    inverse([(fr * gr + fi * gi, fr * gi - fi * gr) for (gr, gi), _ in pairs], (0, 1))
    dh_real, dh_imag = 0.0, 0.0
    for (gr, gi), (ur, ui) in pairs:
        dh_real = dh_real + (gr * ur + gi * ui)
        dh_imag = dh_imag + (gi * ur - gr * ui)
    inverse([(dh_real, dh_imag)], (2,))


VMEM = pl.BlockSpec(memory_space=pltpu.VMEM)
HBM = pl.BlockSpec(memory_space=pltpu.HBM)
SMEM = pl.BlockSpec(memory_space=pltpu.SMEM)
PARAMS = pltpu.CompilerParams(vmem_limit_bytes=32 * 1024 * 1024)


def f32(*shape):
    return jax.ShapeDtypeStruct(shape, jnp.float32)


def shift_x(value, shift):
    return lax.ppermute(value, "x", [(i, (i + shift) % X) for i in range(X)])


def swap_core(value):
    return lax.ppermute(value, "c", [(0, 1), (1, 0)])


def pair_y(value, partner):
    return lax.ppermute(value, "y", [(i, partner(i)) for i in range(Y)])


def per_device(out_grad, conv_input, filter_taps, skip_gain):
    place = class_of(lax.axis_index("x"), lax.axis_index("c"))

    def mine(table):
        return lax.dynamic_index_in_dim(jnp.asarray(table), place, 0, keepdims=False)

    tile = (SUB, LANES)
    scalar = place.reshape(1)
    matrix = right_table()
    right = jnp.asarray(np.stack(numpy_split(matrix) + numpy_split(matrix.T)))

    packed = pl.pallas_call(
        pack_kernel,
        out_shape=pltpu.VMEM((Z, ROWS_IN, *tile), jnp.float32),
        in_specs=[SMEM] + [HBM] * 3,
        out_specs=VMEM,
        scratch_shapes=[
            pltpu.VMEM((Z * 2, SUB * LANES), jnp.float32),
            pltpu.VMEM((Z * 2, SUB * LANES), jnp.float32),
            pltpu.VMEM(tile, jnp.float32),
            pltpu.SemaphoreType.DMA((3,)),
        ],
        compiler_params=pltpu.CompilerParams(vmem_limit_bytes=60 * 1024 * 1024),
    )(scalar, out_grad, conv_input, filter_taps.reshape(tile))
    blocks = lax.all_to_all(packed, "z", 0, 0, tiled=True)

    def z_forward(half):
        return pl.pallas_call(
            functools.partial(z_forward_kernel, half),
            out_shape=f32(X, ROWS_IN, 2, *tile),
            in_specs=[SMEM, VMEM],
            out_specs=VMEM,
            compiler_params=PARAMS,
        )(scalar, blocks)

    sent = z_forward(1)
    first = swap_core(sent[0])
    crossed = swap_core(sent[1:])
    kept = z_forward(0)
    chunks = [jnp.stack([kept[0], first])] + [jnp.stack([kept[i], crossed[i - 1]]) for i in range(1, X)]
    place, chunks[X - 1] = lax.optimization_barrier((place, chunks[X - 1]))
    matrix, back = left_tables(ORDER_IN), np.swapaxes(left_tables(ORDER_OUT), 1, 2)
    left = mine(np.stack(numpy_split(matrix) + numpy_split(back), axis=1))
    twiddle = mine(twiddle_tables())
    chunks = [shift_x(chunk, s) if s else chunk for chunk, s in zip(chunks, ORDER_IN)]
    chunks = pl.pallas_call(
        spectral_kernel,
        out_shape=[f32(C, ROWS_OUT, 2, *tile)] * X,
        in_specs=[VMEM] * 7,
        out_specs=[VMEM] * X,
        compiler_params=PARAMS,
    )(*chunks, left, twiddle, right)
    chunks = [shift_x(chunk, -s) if s else chunk for chunk, s in zip(chunks, ORDER_OUT)]
    own = jnp.stack([chunk[0] for chunk in chunks])
    other = swap_core(jnp.stack([chunk[1] for chunk in chunks]))

    partial, skipped = pl.pallas_call(
        z_inverse_own_kernel,
        out_shape=[f32(Z, ROWS_OUT, *tile), f32(Z, 2, *tile)],
        in_specs=[SMEM, SMEM, VMEM, VMEM],
        out_specs=[VMEM] * 2,
        compiler_params=PARAMS,
    )(scalar, skip_gain, own, packed)
    blocks = pl.pallas_call(
        z_inverse_other_kernel,
        out_shape=f32(Z, ROWS_OUT, *tile),
        in_specs=[SMEM, VMEM, VMEM],
        out_specs=VMEM,
        compiler_params=PARAMS,
    )(scalar, other, partial)
    blocks = lax.all_to_all(blocks, "z", 0, 0, tiled=True)
    filter_grad = jnp.sum(blocks[:, 2], axis=0)
    across = pair_y(filter_grad, lambda i: i ^ 2)
    far = pair_y(filter_grad, lambda i: Y - 1 - i)
    near = pair_y(filter_grad, lambda i: i ^ 1)
    filter_grad = (filter_grad + near) + (far + across)
    input_grad = blocks[:, :2] + skipped
    return (input_grad.reshape(out_grad.shape), filter_grad.reshape(filter_taps.shape))


def solution(mesh):
    fine = Mesh(mesh.devices.reshape(Y, Z, X, C), ("y", "z", "x", "c"))
    return jax.shard_map(
        per_device,
        mesh=fine,
        in_specs=(P("y", None, ("z", "x", "c")), P("y", None, ("z", "x", "c")), P(("z", "x", "c")), P()),
        out_specs=(P("y", None, ("z", "x", "c")), P(("z", "x", "c"))),
        check_vma=False,
    )
```

```python
import functools
import math

import jax
import jax.numpy as jnp
import ml_dtypes
import numpy as np
from jax import lax
from jax.experimental import pallas as pl
from jax.experimental.pallas import tpu as pltpu
from jax.sharding import Mesh, PartitionSpec as P

Y, Z, X, C = 4, 8, 4, 2
ROWS_IN, ROWS_OUT = 5, 3
SHIFTS, SHIFTS_BACK = ((3, 6, 1, 0), (4, 5, 2, 7)), ((1, 6, 3, 0), (2, 5, 4, 7))
KEPT, UNUSED = 3, 7
ORDER_IN, ORDER_OUT = (2, 0, 1, 3), (0, 2, 1, 3)
SUB, LANES = 16, 128
POINTS = 128
SCALE = 1.0 / 131072.0


def class_of(x, c):
    return 2 * x + c


def came_from(zone, core, shifts):
    shift = jnp.where(core == 0, *shifts)
    return (zone - shift) & (Z - 1)


def turn(source, multiple):
    real, imag = jnp.float32(1.0), jnp.float32(0.0)
    for z in range(1, Z):
        angle = math.pi * multiple * z / 16.0
        real = jnp.where(source == z, jnp.float32(math.cos(angle)), real)
        imag = jnp.where(source == z, jnp.float32(-math.sin(angle)), imag)
    return real, imag


def slot_of(x, place, order):
    shift = (x - place // 2) & (X - 1)
    slot = jnp.int32(order.index(0))
    for other in range(1, X):
        slot = jnp.where(shift == other, order.index(other), slot)
    return slot


def numpy_split(table):
    table = table.astype(np.float32)
    high = table.astype(ml_dtypes.bfloat16)
    low = (table - high.astype(np.float32)).astype(ml_dtypes.bfloat16)
    return high, low


def left_tables(order):
    out = np.zeros((X * C, 2, POINTS, X, C, 2, SUB))
    alpha = np.arange(POINTS)[:, None]
    for x in range(X):
        for c in range(C):
            k = class_of(x, c) + 0.5
            for slot, shift in enumerate(order):
                for other in range(C):
                    p = class_of((x - shift) % X, c ^ other)
                    a = p * SUB + np.arange(SUB)[None, :]
                    angle = -2.0 * np.pi * ((a * alpha % POINTS) / POINTS + a * k / 2048.0)
                    at = out[class_of(x, c), :, :, slot, other]
                    at[0, :, 0], at[0, :, 1] = np.cos(angle), -np.sin(angle)
                    at[1, :, 0], at[1, :, 1] = np.sin(angle), np.cos(angle)
    return out.reshape(X * C, 2 * POINTS, 2 * POINTS)


def twiddle_tables():
    out = np.zeros((X * C, 2, POINTS, LANES))
    alpha, b = np.arange(POINTS)[:, None], np.arange(LANES)[None, :]
    for p in range(X * C):
        angle = -2.0 * np.pi * b * (alpha + (p + 0.5) / 16.0) / 16384.0
        out[p, 0], out[p, 1] = np.cos(angle), np.sin(angle)
    return out.astype(np.float32)


def right_table():
    b = np.arange(LANES)
    angle = -2.0 * np.pi * (b[:, None] * b[None, :] % LANES) / LANES
    cosine, sine = np.cos(angle), np.sin(angle)
    return np.block([[cosine, sine], [-sine, cosine]])


def pack_kernel(place_ref, grad_hbm, input_hbm, filter_hbm, out_ref, grad_ref, input_ref, filter_ref, sems):
    pairs = ((grad_hbm.at[0], grad_ref), (input_hbm.at[0], input_ref), (filter_hbm, filter_ref))
    copies = [pltpu.make_async_copy(*pair, sems.at[i]) for i, pair in enumerate(pairs)]
    for copy in copies:
        copy.start()
    for first, ref in ((0, grad_ref), (2, input_ref)):
        copies[first // 2].wait()
        values = ref[...].reshape(Z * 2, SUB, LANES)
        for z in range(Z):
            for row in range(2):
                out_ref[z, first + row] = values[2 * z + row]
    copies[2].wait()
    for z in range(Z):
        out_ref[z, 4] = filter_ref[...]


def z_forward_kernel(half, place_ref, zone_ref, m0, m1, m2, m3, out_ref):
    place, steps = place_ref[0], (m0, m1, m2, m3)
    core = place & 1
    parity = core ^ half
    weights, turns = [], []
    for i in range(len(steps)):
        source = came_from(zone_ref[0], core, (SHIFTS[0][i], SHIFTS[1][i]))
        starts = [turn(source, multiple) for multiple in (1, 3)]
        weights.append([
            jnp.full((SUB, LANES), jnp.where(parity == 0, low, high)) for low, high in zip(*starts)
        ])
        turns.append([jnp.full((SUB, LANES), part) for part in turn(source, 4)])
    for x in range(X):
        slot = slot_of(x, place, ORDER_IN)
        for part in range(2):
            for source in range(C):
                total = weights[0][part] * m0[source]
                for weight, ref in zip(weights[1:], steps[1:]):
                    total = total + weight[part] * ref[source]
                out_ref[slot, source ^ half, :, part] = total
        weights = [
            [real * re - imag * im, real * im + imag * re]
            for (real, imag), (re, im) in zip(weights, turns)
        ]


def z_return_kernel(half, place_ref, zone_ref, near_ref, far_ref, out_ref):
    place = place_ref[0]
    core = place & 1
    slots = [slot_of(x, place, ORDER_OUT) for x in range(X)]
    for i in range(Z // 2):
        shift = jnp.where(core == half, SHIFTS_BACK[0][i], SHIFTS_BACK[1][i])
        target = (zone_ref[0] + shift) & (Z - 1)
        starts = [turn(target, multiple) for multiple in (1, 3)]
        weight = [
            jnp.full((SUB, LANES), jnp.where(core == 0, low, high) * SCALE)
            for low, high in zip(*starts)
        ]
        re, im = [jnp.full((SUB, LANES), part) for part in turn(target, 4)]
        totals = [None, None]
        for x in range(X):
            for part in range(2):
                for block, ref in enumerate((near_ref, far_ref)):
                    term = weight[part] * ref[slots[x], :, part]
                    totals[block] = term if totals[block] is None else totals[block] + term
            real, imag = weight
            weight = [real * re - imag * im, real * im + imag * re]
        for block in range(2):
            out_ref[i, block ^ half] = totals[block]


def filter_sum_kernel(r0, r1, r2, r3, other_ref, out_ref):
    pairs = [ref[0, 2] + other_ref[i, 2] for i, ref in enumerate((r0, r1, r2, r3))]
    out_ref[...] = (pairs[0] + pairs[1]) + (pairs[2] + pairs[3])


def finish_kernel(place_ref, zone_ref, skip_ref, packed_ref, r0, r1, r2, r3, other_ref, out_ref):
    core = place_ref[0] & 1
    for half in range(2):
        for i, ref in enumerate((r0, r1, r2, r3)):
            shifts = (SHIFTS_BACK[0][i], SHIFTS_BACK[1][i])
            source = came_from(zone_ref[0], core ^ half, shifts)
            for row in range(2):
                value = other_ref[i, row] if half else ref[0, row]
                out_ref[source, row] = value + skip_ref[2 * source + row] * packed_ref[source, row]


def split(value):
    high = value.astype(jnp.bfloat16)
    return high, (value - high.astype(jnp.float32)).astype(jnp.bfloat16)


def product(left, right):
    (left_high, left_low), (right_high, right_low) = left, right
    dot = functools.partial(jnp.dot, preferred_element_type=jnp.float32)
    return dot(left_high, right_high) + (dot(left_high, right_low) + dot(left_low, right_high))


def spectral_kernel(
    x0, x1, x2, x3, left, tw, right, o0, o1, o2, o3
):
    chunks, outs = (x0, x1, x2, x3), (o0, o1, o2, o3)
    wh, wl, wth, wtl = (left[i] for i in range(4))
    bh, bl, bth, btl = (right[i] for i in range(4))
    pieces = [(s, c, part) for s in range(X) for c in range(C) for part in range(2)]
    cosine, sine = tw[0], tw[1]

    def forward(*picked):
        columns = [
            jnp.concatenate([chunks[s][c, row, part] for s, c, part in pieces], axis=0)
            for row in picked
        ]
        value = product((wh, wl), split(jnp.concatenate(columns, axis=1)))
        rows = []
        for i in range(len(picked)):
            lanes = slice(i * LANES, (i + 1) * LANES)
            real, imag = value[:POINTS, lanes], value[POINTS:, lanes]
            rows.append(
                jnp.concatenate([real * cosine - imag * sine, real * sine + imag * cosine], axis=1)
            )
        value = product(split(jnp.concatenate(rows, axis=0)), (bh, bl))
        spans = [slice(i * POINTS, (i + 1) * POINTS) for i in range(len(picked))]
        return [(value[span, :LANES], value[span, LANES:]) for span in spans]

    def inverse(spectra, picked):
        rows = jnp.concatenate([jnp.concatenate(pair, axis=1) for pair in spectra], axis=0)
        value = product(split(rows), (bth, btl))
        columns = []
        for i in range(len(picked)):
            span = slice(i * POINTS, (i + 1) * POINTS)
            vr, vi = value[span, :LANES], value[span, LANES:]
            columns.append(
                jnp.concatenate([vr * cosine + vi * sine, vi * cosine - vr * sine], axis=0)
            )
        value = product((wth, wtl), split(jnp.concatenate(columns, axis=1)))
        for index, (s, c, part) in enumerate(pieces):
            for i, row in enumerate(picked):
                outs[s][c, row, part] = value[
                    index * SUB : (index + 1) * SUB, i * LANES : (i + 1) * LANES
                ]

    ((fr, fi),) = forward(4)
    pairs = [forward(channel, 2 + channel) for channel in range(2)]
    inverse([(fr * gr + fi * gi, fr * gi - fi * gr) for (gr, gi), _ in pairs], (0, 1))
    dh_real, dh_imag = 0.0, 0.0
    for (gr, gi), (ur, ui) in pairs:
        dh_real = dh_real + (gr * ur + gi * ui)
        dh_imag = dh_imag + (gi * ur - gr * ui)
    inverse([(dh_real, dh_imag)], (2,))


VMEM = pl.BlockSpec(memory_space=pltpu.VMEM)
HBM = pl.BlockSpec(memory_space=pltpu.HBM)
SMEM = pl.BlockSpec(memory_space=pltpu.SMEM)
PARAMS = pltpu.CompilerParams(vmem_limit_bytes=32 * 1024 * 1024)


def f32(*shape):
    return jax.ShapeDtypeStruct(shape, jnp.float32)


def shift_x(value, shift):
    return lax.ppermute(value, "x", [(i, (i + shift) % X) for i in range(X)])


def shift_z(value, even, odd):
    pairs = [(C * z + c, C * ((z + by) % Z) + c) for c, by in enumerate((even, odd)) for z in range(Z)]
    return lax.ppermute(value, ("z", "c"), pairs)


def swap_core(value):
    return lax.ppermute(value, "c", [(0, 1), (1, 0)])


def pair_y(value, partner):
    return lax.ppermute(value, "y", [(i, partner(i)) for i in range(Y)])


def per_device(out_grad, conv_input, filter_taps, skip_gain):
    place = class_of(lax.axis_index("x"), lax.axis_index("c"))

    def mine(table):
        return lax.dynamic_index_in_dim(jnp.asarray(table), place, 0, keepdims=False)

    tile = (SUB, LANES)
    scalar = place.reshape(1)
    matrix = right_table()
    right = jnp.asarray(np.stack(numpy_split(matrix) + numpy_split(matrix.T)))

    packed = pl.pallas_call(
        pack_kernel,
        out_shape=pltpu.VMEM((Z, ROWS_IN, *tile), jnp.float32),
        in_specs=[SMEM] + [HBM] * 3,
        out_specs=VMEM,
        scratch_shapes=[
            pltpu.VMEM((Z * 2, SUB * LANES), jnp.float32),
            pltpu.VMEM((Z * 2, SUB * LANES), jnp.float32),
            pltpu.VMEM(tile, jnp.float32),
            pltpu.SemaphoreType.DMA((3,)),
        ],
        compiler_params=pltpu.CompilerParams(vmem_limit_bytes=60 * 1024 * 1024),
    )(scalar, out_grad, conv_input, filter_taps.reshape(tile))
    zone, core = lax.axis_index("z"), lax.axis_index("c")

    def toward(i, crossed):
        shift = jnp.where(core == crossed, SHIFTS[0][i], SHIFTS[1][i])
        return lax.dynamic_index_in_dim(packed, (zone + shift) & (Z - 1), 0, keepdims=False)

    given = swap_core(jnp.stack([toward(i, 1) for i in range(Z // 2)]))

    def exchange_z(messages, shifts):
        even = shifts[0][:KEPT] + (UNUSED,)
        moved = [shift_z(m, *by) for m, *by in zip(messages, even, shifts[1])]
        moved[KEPT] = jnp.where(core == 0, messages[KEPT], moved[KEPT])
        return moved

    steps = exchange_z([jnp.stack([toward(i, 0), given[i]]) for i in range(Z // 2)], SHIFTS)

    def z_forward(half):
        return pl.pallas_call(
            functools.partial(z_forward_kernel, half),
            out_shape=f32(X, C, ROWS_IN, 2, *tile),
            in_specs=[SMEM, SMEM] + [VMEM] * 4,
            out_specs=VMEM,
            compiler_params=PARAMS,
        )(scalar, zone.reshape(1), *steps)

    sent = z_forward(1)
    first = swap_core(sent[0])
    crossed = swap_core(sent[1:])
    kept = z_forward(0)
    chunks = [kept[0] + first] + [kept[i] + crossed[i - 1] for i in range(1, X)]
    place, chunks[X - 1] = lax.optimization_barrier((place, chunks[X - 1]))
    matrix, back = left_tables(ORDER_IN), np.swapaxes(left_tables(ORDER_OUT), 1, 2)
    left = mine(np.stack(numpy_split(matrix) + numpy_split(back), axis=1))
    twiddle = mine(twiddle_tables())
    chunks = [shift_x(chunk, s) if s else chunk for chunk, s in zip(chunks, ORDER_IN)]
    chunks = pl.pallas_call(
        spectral_kernel,
        out_shape=[f32(C, ROWS_OUT, 2, *tile)] * X,
        in_specs=[VMEM] * 7,
        out_specs=[VMEM] * X,
        compiler_params=PARAMS,
    )(*chunks, left, twiddle, right)
    chunks = [shift_x(chunk, -s) if s else chunk for chunk, s in zip(chunks, ORDER_OUT)]
    near = jnp.stack([chunk[0] for chunk in chunks])
    far = jnp.stack([chunk[1] for chunk in chunks])

    def z_return(half):
        return pl.pallas_call(
            functools.partial(z_return_kernel, half),
            out_shape=f32(Z // 2, C, ROWS_OUT, *tile),
            in_specs=[SMEM] * 2 + [VMEM] * 2,
            out_specs=VMEM,
            compiler_params=PARAMS,
        )(scalar, zone.reshape(1), near, far)

    crossed = swap_core(z_return(1))
    kept = z_return(0)
    steps = exchange_z([kept[i] + crossed[i] for i in range(Z // 2)], SHIFTS_BACK)
    others = swap_core(jnp.stack([step[1] for step in steps]))
    filter_grad = pl.pallas_call(
        filter_sum_kernel,
        out_shape=f32(*tile),
        in_specs=[VMEM] * 5,
        out_specs=VMEM,
        compiler_params=PARAMS,
    )(*steps, others)
    input_grad = pl.pallas_call(
        finish_kernel,
        out_shape=f32(Z, 2, *tile),
        in_specs=[SMEM] * 3 + [VMEM] * 6,
        out_specs=VMEM,
        compiler_params=PARAMS,
    )(scalar, zone.reshape(1), skip_gain, packed, *steps, others)
    across = pair_y(filter_grad, lambda i: i ^ 2)
    far = pair_y(filter_grad, lambda i: Y - 1 - i)
    near = pair_y(filter_grad, lambda i: i ^ 1)
    filter_grad = (filter_grad + near) + (far + across)
    return (input_grad.reshape(out_grad.shape), filter_grad.reshape(filter_taps.shape))


def solution(mesh):
    fine = Mesh(mesh.devices.reshape(Y, Z, X, C), ("y", "z", "x", "c"))
    return jax.shard_map(
        per_device,
        mesh=fine,
        in_specs=(P("y", None, ("z", "x", "c")), P("y", None, ("z", "x", "c")), P(("z", "x", "c")), P()),
        out_specs=(P("y", None, ("z", "x", "c")), P(("z", "x", "c"))),
        check_vma=False,
    )
```

```python
import functools
import math

import jax
import jax.numpy as jnp
import ml_dtypes
import numpy as np
from jax import lax
from jax.experimental import pallas as pl
from jax.experimental.pallas import tpu as pltpu
from jax.sharding import Mesh, PartitionSpec as P

Y, Z, X, C = 4, 8, 4, 2
ROWS_IN, ROWS_OUT = 5, 3
SHIFTS, SHIFTS_BACK = ((3, 6, 1, 0), (5, 2, 7, 4)), ((1, 6, 3, 0), (7, 2, 5, 4))
KEPT, UNUSED = 3, 7
ORDER_IN, ORDER_OUT = (2, 0, 1, 3), (0, 2, 1, 3)
SUB, LANES = 16, 128
POINTS = 128
SCALE = 1.0 / 131072.0


def class_of(x, c):
    return 2 * x + c


def came_from(zone, core, shifts):
    shift = jnp.where(core == 0, *shifts)
    return (zone - shift) & (Z - 1)


def turn(source, multiple):
    real, imag = jnp.float32(1.0), jnp.float32(0.0)
    for z in range(1, Z):
        angle = math.pi * multiple * z / 16.0
        real = jnp.where(source == z, jnp.float32(math.cos(angle)), real)
        imag = jnp.where(source == z, jnp.float32(-math.sin(angle)), imag)
    return real, imag


def slot_of(x, place, order):
    shift = (x - place // 2) & (X - 1)
    slot = jnp.int32(order.index(0))
    for other in range(1, X):
        slot = jnp.where(shift == other, order.index(other), slot)
    return slot


def numpy_split(table):
    table = table.astype(np.float32)
    high = table.astype(ml_dtypes.bfloat16)
    low = (table - high.astype(np.float32)).astype(ml_dtypes.bfloat16)
    return high, low


def left_tables(order):
    out = np.zeros((X * C, 2, POINTS, X, C, 2, SUB))
    alpha = np.arange(POINTS)[:, None]
    for x in range(X):
        for c in range(C):
            k = class_of(x, c) + 0.5
            for slot, shift in enumerate(order):
                for other in range(C):
                    p = class_of((x - shift) % X, c ^ other)
                    a = p * SUB + np.arange(SUB)[None, :]
                    angle = -2.0 * np.pi * ((a * alpha % POINTS) / POINTS + a * k / 2048.0)
                    at = out[class_of(x, c), :, :, slot, other]
                    at[0, :, 0], at[0, :, 1] = np.cos(angle), -np.sin(angle)
                    at[1, :, 0], at[1, :, 1] = np.sin(angle), np.cos(angle)
    return out.reshape(X * C, 2 * POINTS, 2 * POINTS)


def twiddle_tables():
    out = np.zeros((X * C, 2, POINTS, LANES))
    alpha, b = np.arange(POINTS)[:, None], np.arange(LANES)[None, :]
    for p in range(X * C):
        angle = -2.0 * np.pi * b * (alpha + (p + 0.5) / 16.0) / 16384.0
        out[p, 0], out[p, 1] = np.cos(angle), np.sin(angle)
    return out.astype(np.float32)


def right_table():
    b = np.arange(LANES)
    angle = -2.0 * np.pi * (b[:, None] * b[None, :] % LANES) / LANES
    cosine, sine = np.cos(angle), np.sin(angle)
    return np.block([[cosine, sine], [-sine, cosine]])


def pack_kernel(place_ref, grad_hbm, input_hbm, filter_hbm, out_ref, grad_ref, input_ref, filter_ref, sems):
    pairs = ((grad_hbm.at[0], grad_ref), (input_hbm.at[0], input_ref), (filter_hbm, filter_ref))
    copies = [pltpu.make_async_copy(*pair, sems.at[i]) for i, pair in enumerate(pairs)]
    for copy in copies:
        copy.start()
    for first, ref in ((0, grad_ref), (2, input_ref)):
        copies[first // 2].wait()
        values = ref[...].reshape(Z * 2, SUB, LANES)
        for z in range(Z):
            for row in range(2):
                out_ref[z, first + row] = values[2 * z + row]
    copies[2].wait()
    for z in range(Z):
        out_ref[z, 4] = filter_ref[...]


def z_forward_kernel(half, place_ref, zone_ref, m0, m1, m2, m3, out_ref):
    place, steps = place_ref[0], (m0, m1, m2, m3)
    core = place & 1
    parity = core ^ half
    weights, turns = [], []
    for i in range(len(steps)):
        source = came_from(zone_ref[0], core, (SHIFTS[0][i], SHIFTS[1][i]))
        starts = [turn(source, multiple) for multiple in (1, 3)]
        weights.append([
            jnp.full((SUB, LANES), jnp.where(parity == 0, low, high)) for low, high in zip(*starts)
        ])
        turns.append([jnp.full((SUB, LANES), part) for part in turn(source, 4)])
    for x in range(X):
        slot = slot_of(x, place, ORDER_IN)
        for part in range(2):
            for source in range(C):
                total = weights[0][part] * m0[source]
                for weight, ref in zip(weights[1:], steps[1:]):
                    total = total + weight[part] * ref[source]
                out_ref[slot, source ^ half, :, part] = total
        weights = [
            [real * re - imag * im, real * im + imag * re]
            for (real, imag), (re, im) in zip(weights, turns)
        ]


def z_return_kernel(half, place_ref, zone_ref, near_ref, far_ref, out_ref):
    place = place_ref[0]
    core = place & 1
    slots = [slot_of(x, place, ORDER_OUT) for x in range(X)]
    for i in range(Z // 2):
        shift = jnp.where(core == half, SHIFTS_BACK[0][i], SHIFTS_BACK[1][i])
        target = (zone_ref[0] + shift) & (Z - 1)
        starts = [turn(target, multiple) for multiple in (1, 3)]
        weight = [
            jnp.full((SUB, LANES), jnp.where(core == 0, low, high) * SCALE)
            for low, high in zip(*starts)
        ]
        re, im = [jnp.full((SUB, LANES), part) for part in turn(target, 4)]
        totals = [None, None]
        for x in range(X):
            for part in range(2):
                for block, ref in enumerate((near_ref, far_ref)):
                    term = weight[part] * ref[slots[x], :, part]
                    totals[block] = term if totals[block] is None else totals[block] + term
            real, imag = weight
            weight = [real * re - imag * im, real * im + imag * re]
        for block in range(2):
            out_ref[i, block ^ half] = totals[block]


def filter_sum_kernel(r0, r1, r2, r3, other_ref, out_ref):
    pairs = [ref[0, 2] + other_ref[i, 2] for i, ref in enumerate((r0, r1, r2, r3))]
    out_ref[...] = (pairs[0] + pairs[1]) + (pairs[2] + pairs[3])


def finish_kernel(place_ref, zone_ref, skip_ref, packed_ref, r0, r1, r2, r3, other_ref, out_ref):
    core = place_ref[0] & 1
    for half in range(2):
        for i, ref in enumerate((r0, r1, r2, r3)):
            shifts = (SHIFTS_BACK[0][i], SHIFTS_BACK[1][i])
            source = came_from(zone_ref[0], core ^ half, shifts)
            for row in range(2):
                value = other_ref[i, row] if half else ref[0, row]
                out_ref[source, row] = value + skip_ref[2 * source + row] * packed_ref[source, row]


def split(value):
    high = value.astype(jnp.bfloat16)
    return high, (value - high.astype(jnp.float32)).astype(jnp.bfloat16)


def product(left, right):
    (left_high, left_low), (right_high, right_low) = left, right
    dot = functools.partial(jnp.dot, preferred_element_type=jnp.float32)
    return dot(left_high, right_high) + (dot(left_high, right_low) + dot(left_low, right_high))


def spectral_kernel(
    x0, x1, x2, x3, left, tw, right, o0, o1, o2, o3
):
    chunks, outs = (x0, x1, x2, x3), (o0, o1, o2, o3)
    wh, wl, wth, wtl = (left[i] for i in range(4))
    bh, bl, bth, btl = (right[i] for i in range(4))
    pieces = [(s, c, part) for s in range(X) for c in range(C) for part in range(2)]
    cosine, sine = tw[0], tw[1]

    def forward(*picked):
        columns = [
            jnp.concatenate([chunks[s][c, row, part] for s, c, part in pieces], axis=0)
            for row in picked
        ]
        value = product((wh, wl), split(jnp.concatenate(columns, axis=1)))
        rows = []
        for i in range(len(picked)):
            lanes = slice(i * LANES, (i + 1) * LANES)
            real, imag = value[:POINTS, lanes], value[POINTS:, lanes]
            rows.append(
                jnp.concatenate([real * cosine - imag * sine, real * sine + imag * cosine], axis=1)
            )
        value = product(split(jnp.concatenate(rows, axis=0)), (bh, bl))
        spans = [slice(i * POINTS, (i + 1) * POINTS) for i in range(len(picked))]
        return [(value[span, :LANES], value[span, LANES:]) for span in spans]

    def inverse(spectra, picked):
        rows = jnp.concatenate([jnp.concatenate(pair, axis=1) for pair in spectra], axis=0)
        value = product(split(rows), (bth, btl))
        columns = []
        for i in range(len(picked)):
            span = slice(i * POINTS, (i + 1) * POINTS)
            vr, vi = value[span, :LANES], value[span, LANES:]
            columns.append(
                jnp.concatenate([vr * cosine + vi * sine, vi * cosine - vr * sine], axis=0)
            )
        value = product((wth, wtl), split(jnp.concatenate(columns, axis=1)))
        for index, (s, c, part) in enumerate(pieces):
            for i, row in enumerate(picked):
                outs[s][c, row, part] = value[
                    index * SUB : (index + 1) * SUB, i * LANES : (i + 1) * LANES
                ]

    ((fr, fi),) = forward(4)
    pairs = [forward(channel, 2 + channel) for channel in range(2)]
    inverse([(fr * gr + fi * gi, fr * gi - fi * gr) for (gr, gi), _ in pairs], (0, 1))
    dh_real, dh_imag = 0.0, 0.0
    for (gr, gi), (ur, ui) in pairs:
        dh_real = dh_real + (gr * ur + gi * ui)
        dh_imag = dh_imag + (gi * ur - gr * ui)
    inverse([(dh_real, dh_imag)], (2,))


VMEM = pl.BlockSpec(memory_space=pltpu.VMEM)
HBM = pl.BlockSpec(memory_space=pltpu.HBM)
SMEM = pl.BlockSpec(memory_space=pltpu.SMEM)
PARAMS = pltpu.CompilerParams(vmem_limit_bytes=32 * 1024 * 1024)


def f32(*shape):
    return jax.ShapeDtypeStruct(shape, jnp.float32)


def shift_x(value, shift):
    return lax.ppermute(value, "x", [(i, (i + shift) % X) for i in range(X)])


def shift_z(value, even, odd):
    pairs = [(C * z + c, C * ((z + by) % Z) + c) for c, by in enumerate((even, odd)) for z in range(Z)]
    return lax.ppermute(value, ("z", "c"), pairs)


def swap_core(value):
    return lax.ppermute(value, "c", [(0, 1), (1, 0)])


def pair_y(value, partner):
    return lax.ppermute(value, "y", [(i, partner(i)) for i in range(Y)])


def per_device(out_grad, conv_input, filter_taps, skip_gain):
    place = class_of(lax.axis_index("x"), lax.axis_index("c"))

    def mine(table):
        return lax.dynamic_index_in_dim(jnp.asarray(table), place, 0, keepdims=False)

    tile = (SUB, LANES)
    scalar = place.reshape(1)
    matrix = right_table()
    right = jnp.asarray(np.stack(numpy_split(matrix) + numpy_split(matrix.T)))

    packed = pl.pallas_call(
        pack_kernel,
        out_shape=pltpu.VMEM((Z, ROWS_IN, *tile), jnp.float32),
        in_specs=[SMEM] + [HBM] * 3,
        out_specs=VMEM,
        scratch_shapes=[
            pltpu.VMEM((Z * 2, SUB * LANES), jnp.float32),
            pltpu.VMEM((Z * 2, SUB * LANES), jnp.float32),
            pltpu.VMEM(tile, jnp.float32),
            pltpu.SemaphoreType.DMA((3,)),
        ],
        compiler_params=pltpu.CompilerParams(vmem_limit_bytes=60 * 1024 * 1024),
    )(scalar, out_grad, conv_input, filter_taps.reshape(tile))
    zone, core = lax.axis_index("z"), lax.axis_index("c")

    def toward(i, crossed):
        shift = jnp.where(core == crossed, SHIFTS[0][i], SHIFTS[1][i])
        return lax.dynamic_index_in_dim(packed, (zone + shift) & (Z - 1), 0, keepdims=False)

    given = swap_core(jnp.stack([toward(i, 1) for i in range(Z // 2)]))

    def exchange_z(messages, shifts):
        even = shifts[0][:KEPT] + (UNUSED,)
        moved = [shift_z(m, *by) for m, *by in zip(messages, even, shifts[1])]
        moved[KEPT] = jnp.where(core == 0, messages[KEPT], moved[KEPT])
        return moved

    steps = exchange_z([jnp.stack([toward(i, 0), given[i]]) for i in range(Z // 2)], SHIFTS)

    def z_forward(half):
        return pl.pallas_call(
            functools.partial(z_forward_kernel, half),
            out_shape=f32(X, C, ROWS_IN, 2, *tile),
            in_specs=[SMEM, SMEM] + [VMEM] * 4,
            out_specs=VMEM,
            compiler_params=PARAMS,
        )(scalar, zone.reshape(1), *steps)

    sent = z_forward(1)
    first = swap_core(sent[0])
    crossed = swap_core(sent[1:])
    kept = z_forward(0)
    chunks = [kept[0] + first] + [kept[i] + crossed[i - 1] for i in range(1, X)]
    place, chunks[X - 1] = lax.optimization_barrier((place, chunks[X - 1]))
    matrix, back = left_tables(ORDER_IN), np.swapaxes(left_tables(ORDER_OUT), 1, 2)
    left = mine(np.stack(numpy_split(matrix) + numpy_split(back), axis=1))
    twiddle = mine(twiddle_tables())
    chunks = [shift_x(chunk, s) if s else chunk for chunk, s in zip(chunks, ORDER_IN)]
    chunks = pl.pallas_call(
        spectral_kernel,
        out_shape=[f32(C, ROWS_OUT, 2, *tile)] * X,
        in_specs=[VMEM] * 7,
        out_specs=[VMEM] * X,
        compiler_params=PARAMS,
    )(*chunks, left, twiddle, right)
    chunks = [shift_x(chunk, -s) if s else chunk for chunk, s in zip(chunks, ORDER_OUT)]
    near = jnp.stack([chunk[0] for chunk in chunks])
    far = jnp.stack([chunk[1] for chunk in chunks])

    def z_return(half):
        return pl.pallas_call(
            functools.partial(z_return_kernel, half),
            out_shape=f32(Z // 2, C, ROWS_OUT, *tile),
            in_specs=[SMEM] * 2 + [VMEM] * 2,
            out_specs=VMEM,
            compiler_params=PARAMS,
        )(scalar, zone.reshape(1), near, far)

    crossed = swap_core(z_return(1))
    kept = z_return(0)
    steps = exchange_z([kept[i] + crossed[i] for i in range(Z // 2)], SHIFTS_BACK)
    others = swap_core(jnp.stack([step[1] for step in steps]))
    filter_grad = pl.pallas_call(
        filter_sum_kernel,
        out_shape=f32(*tile),
        in_specs=[VMEM] * 5,
        out_specs=VMEM,
        compiler_params=PARAMS,
    )(*steps, others)
    input_grad = pl.pallas_call(
        finish_kernel,
        out_shape=f32(Z, 2, *tile),
        in_specs=[SMEM] * 3 + [VMEM] * 6,
        out_specs=VMEM,
        compiler_params=PARAMS,
    )(scalar, zone.reshape(1), skip_gain, packed, *steps, others)
    across = pair_y(filter_grad, lambda i: i ^ 2)
    far = pair_y(filter_grad, lambda i: Y - 1 - i)
    near = pair_y(filter_grad, lambda i: i ^ 1)
    filter_grad = (filter_grad + near) + (far + across)
    return (input_grad.reshape(out_grad.shape), filter_grad.reshape(filter_taps.shape))


def solution(mesh):
    fine = Mesh(mesh.devices.reshape(Y, Z, X, C), ("y", "z", "x", "c"))
    return jax.shard_map(
        per_device,
        mesh=fine,
        in_specs=(P("y", None, ("z", "x", "c")), P("y", None, ("z", "x", "c")), P(("z", "x", "c")), P()),
        out_specs=(P("y", None, ("z", "x", "c")), P(("z", "x", "c"))),
        check_vma=False,
    )
```

```python
import functools
import math

import jax
import jax.numpy as jnp
import ml_dtypes
import numpy as np
from jax import lax
from jax.experimental import pallas as pl
from jax.experimental.pallas import tpu as pltpu
from jax.sharding import Mesh, PartitionSpec as P

Y, Z, X, C = 4, 8, 4, 2
ROWS_IN, ROWS_OUT = 5, 3
SHIFTS, SHIFTS_BACK = ((3, 1, 6, 0), (5, 7, 2, 4)), ((1, 6, 3, 0), (7, 2, 5, 4))
KEPT, UNUSED = 3, 7
ORDER_IN, ORDER_OUT = (2, 0, 1, 3), (0, 2, 1, 3)
SUB, LANES = 16, 128
POINTS = 128
SCALE = 1.0 / 131072.0


def class_of(x, c):
    return 2 * x + c


def came_from(zone, core, shifts):
    shift = jnp.where(core == 0, *shifts)
    return (zone - shift) & (Z - 1)


def turn(source, multiple):
    real, imag = jnp.float32(1.0), jnp.float32(0.0)
    for z in range(1, Z):
        angle = math.pi * multiple * z / 16.0
        real = jnp.where(source == z, jnp.float32(math.cos(angle)), real)
        imag = jnp.where(source == z, jnp.float32(-math.sin(angle)), imag)
    return real, imag


def slot_of(x, place, order):
    shift = (x - place // 2) & (X - 1)
    slot = jnp.int32(order.index(0))
    for other in range(1, X):
        slot = jnp.where(shift == other, order.index(other), slot)
    return slot


def numpy_split(table):
    table = table.astype(np.float32)
    high = table.astype(ml_dtypes.bfloat16)
    low = (table - high.astype(np.float32)).astype(ml_dtypes.bfloat16)
    return high, low


def left_tables(order):
    out = np.zeros((X * C, 2, POINTS, X, C, 2, SUB))
    alpha = np.arange(POINTS)[:, None]
    for x in range(X):
        for c in range(C):
            k = class_of(x, c) + 0.5
            for slot, shift in enumerate(order):
                for other in range(C):
                    p = class_of((x - shift) % X, c ^ other)
                    a = p * SUB + np.arange(SUB)[None, :]
                    angle = -2.0 * np.pi * ((a * alpha % POINTS) / POINTS + a * k / 2048.0)
                    at = out[class_of(x, c), :, :, slot, other]
                    at[0, :, 0], at[0, :, 1] = np.cos(angle), -np.sin(angle)
                    at[1, :, 0], at[1, :, 1] = np.sin(angle), np.cos(angle)
    return out.reshape(X * C, 2 * POINTS, 2 * POINTS)


def twiddle_tables():
    out = np.zeros((X * C, 2, POINTS, LANES))
    alpha, b = np.arange(POINTS)[:, None], np.arange(LANES)[None, :]
    for p in range(X * C):
        angle = -2.0 * np.pi * b * (alpha + (p + 0.5) / 16.0) / 16384.0
        out[p, 0], out[p, 1] = np.cos(angle), np.sin(angle)
    return out.astype(np.float32)


def right_table():
    b = np.arange(LANES)
    angle = -2.0 * np.pi * (b[:, None] * b[None, :] % LANES) / LANES
    cosine, sine = np.cos(angle), np.sin(angle)
    return np.block([[cosine, sine], [-sine, cosine]])


def pack_kernel(place_ref, grad_hbm, input_hbm, filter_hbm, out_ref, grad_ref, input_ref, filter_ref, sems):
    pairs = ((grad_hbm.at[0], grad_ref), (input_hbm.at[0], input_ref), (filter_hbm, filter_ref))
    copies = [pltpu.make_async_copy(*pair, sems.at[i]) for i, pair in enumerate(pairs)]
    for copy in copies:
        copy.start()
    for first, ref in ((0, grad_ref), (2, input_ref)):
        copies[first // 2].wait()
        values = ref[...].reshape(Z * 2, SUB, LANES)
        for z in range(Z):
            for row in range(2):
                out_ref[z, first + row] = values[2 * z + row]
    copies[2].wait()
    for z in range(Z):
        out_ref[z, 4] = filter_ref[...]


def z_forward_kernel(half, place_ref, zone_ref, m0, m1, m2, m3, out_ref):
    place, steps = place_ref[0], (m0, m1, m2, m3)
    core = place & 1
    parity = core ^ half
    weights, turns = [], []
    for i in range(len(steps)):
        source = came_from(zone_ref[0], core, (SHIFTS[0][i], SHIFTS[1][i]))
        starts = [turn(source, multiple) for multiple in (1, 3)]
        weights.append([
            jnp.full((SUB, LANES), jnp.where(parity == 0, low, high)) for low, high in zip(*starts)
        ])
        turns.append([jnp.full((SUB, LANES), part) for part in turn(source, 4)])
    for x in range(X):
        slot = slot_of(x, place, ORDER_IN)
        for part in range(2):
            for source in range(C):
                total = weights[0][part] * m0[source]
                for weight, ref in zip(weights[1:], steps[1:]):
                    total = total + weight[part] * ref[source]
                out_ref[slot, source ^ half, :, part] = total
        weights = [
            [real * re - imag * im, real * im + imag * re]
            for (real, imag), (re, im) in zip(weights, turns)
        ]


def z_return_kernel(half, place_ref, zone_ref, near_ref, far_ref, out_ref):
    place = place_ref[0]
    core = place & 1
    slots = [slot_of(x, place, ORDER_OUT) for x in range(X)]
    for i in range(Z // 2):
        shift = jnp.where(core == half, SHIFTS_BACK[0][i], SHIFTS_BACK[1][i])
        target = (zone_ref[0] + shift) & (Z - 1)
        starts = [turn(target, multiple) for multiple in (1, 3)]
        weight = [
            jnp.full((SUB, LANES), jnp.where(core == 0, low, high) * SCALE)
            for low, high in zip(*starts)
        ]
        re, im = [jnp.full((SUB, LANES), part) for part in turn(target, 4)]
        totals = [None, None]
        for x in range(X):
            for part in range(2):
                for block, ref in enumerate((near_ref, far_ref)):
                    term = weight[part] * ref[slots[x], :, part]
                    totals[block] = term if totals[block] is None else totals[block] + term
            real, imag = weight
            weight = [real * re - imag * im, real * im + imag * re]
        for block in range(2):
            out_ref[i, block ^ half] = totals[block]


def filter_sum_kernel(r0, r1, r2, r3, other_ref, out_ref):
    pairs = [ref[0, 2] + other_ref[i, 2] for i, ref in enumerate((r0, r1, r2, r3))]
    out_ref[...] = (pairs[0] + pairs[1]) + (pairs[2] + pairs[3])


def finish_kernel(place_ref, zone_ref, skip_ref, packed_ref, r0, r1, r2, r3, other_ref, out_ref):
    core = place_ref[0] & 1
    for half in range(2):
        for i, ref in enumerate((r0, r1, r2, r3)):
            shifts = (SHIFTS_BACK[0][i], SHIFTS_BACK[1][i])
            source = came_from(zone_ref[0], core ^ half, shifts)
            for row in range(2):
                value = other_ref[i, row] if half else ref[0, row]
                out_ref[source, row] = value + skip_ref[2 * source + row] * packed_ref[source, row]


def split(value):
    high = value.astype(jnp.bfloat16)
    return high, (value - high.astype(jnp.float32)).astype(jnp.bfloat16)


def product(left, right):
    (left_high, left_low), (right_high, right_low) = left, right
    dot = functools.partial(jnp.dot, preferred_element_type=jnp.float32)
    return dot(left_high, right_high) + (dot(left_high, right_low) + dot(left_low, right_high))


def spectral_kernel(
    x0, x1, x2, x3, left, tw, right, o0, o1, o2, o3
):
    chunks, outs = (x0, x1, x2, x3), (o0, o1, o2, o3)
    wh, wl, wth, wtl = (left[i] for i in range(4))
    bh, bl, bth, btl = (right[i] for i in range(4))
    pieces = [(s, c, part) for s in range(X) for c in range(C) for part in range(2)]
    cosine, sine = tw[0], tw[1]

    def forward(*picked):
        columns = [
            jnp.concatenate([chunks[s][c, row, part] for s, c, part in pieces], axis=0)
            for row in picked
        ]
        value = product((wh, wl), split(jnp.concatenate(columns, axis=1)))
        rows = []
        for i in range(len(picked)):
            lanes = slice(i * LANES, (i + 1) * LANES)
            real, imag = value[:POINTS, lanes], value[POINTS:, lanes]
            rows.append(
                jnp.concatenate([real * cosine - imag * sine, real * sine + imag * cosine], axis=1)
            )
        value = product(split(jnp.concatenate(rows, axis=0)), (bh, bl))
        spans = [slice(i * POINTS, (i + 1) * POINTS) for i in range(len(picked))]
        return [(value[span, :LANES], value[span, LANES:]) for span in spans]

    def inverse(spectra, picked):
        rows = jnp.concatenate([jnp.concatenate(pair, axis=1) for pair in spectra], axis=0)
        value = product(split(rows), (bth, btl))
        columns = []
        for i in range(len(picked)):
            span = slice(i * POINTS, (i + 1) * POINTS)
            vr, vi = value[span, :LANES], value[span, LANES:]
            columns.append(
                jnp.concatenate([vr * cosine + vi * sine, vi * cosine - vr * sine], axis=0)
            )
        value = product((wth, wtl), split(jnp.concatenate(columns, axis=1)))
        for index, (s, c, part) in enumerate(pieces):
            for i, row in enumerate(picked):
                outs[s][c, row, part] = value[
                    index * SUB : (index + 1) * SUB, i * LANES : (i + 1) * LANES
                ]

    ((fr, fi),) = forward(4)
    pairs = [forward(channel, 2 + channel) for channel in range(2)]
    inverse([(fr * gr + fi * gi, fr * gi - fi * gr) for (gr, gi), _ in pairs], (0, 1))
    dh_real, dh_imag = 0.0, 0.0
    for (gr, gi), (ur, ui) in pairs:
        dh_real = dh_real + (gr * ur + gi * ui)
        dh_imag = dh_imag + (gi * ur - gr * ui)
    inverse([(dh_real, dh_imag)], (2,))


VMEM = pl.BlockSpec(memory_space=pltpu.VMEM)
HBM = pl.BlockSpec(memory_space=pltpu.HBM)
SMEM = pl.BlockSpec(memory_space=pltpu.SMEM)
PARAMS = pltpu.CompilerParams(vmem_limit_bytes=32 * 1024 * 1024)


def f32(*shape):
    return jax.ShapeDtypeStruct(shape, jnp.float32)


def shift_x(value, shift):
    return lax.ppermute(value, "x", [(i, (i + shift) % X) for i in range(X)])


def shift_z(value, even, odd):
    pairs = [(C * z + c, C * ((z + by) % Z) + c) for c, by in enumerate((even, odd)) for z in range(Z)]
    return lax.ppermute(value, ("z", "c"), pairs)


def swap_core(value):
    return lax.ppermute(value, "c", [(0, 1), (1, 0)])


def pair_y(value, partner):
    return lax.ppermute(value, "y", [(i, partner(i)) for i in range(Y)])


def per_device(out_grad, conv_input, filter_taps, skip_gain):
    place = class_of(lax.axis_index("x"), lax.axis_index("c"))

    def mine(table):
        return lax.dynamic_index_in_dim(jnp.asarray(table), place, 0, keepdims=False)

    tile = (SUB, LANES)
    scalar = place.reshape(1)
    matrix = right_table()
    right = jnp.asarray(np.stack(numpy_split(matrix) + numpy_split(matrix.T)))

    packed = pl.pallas_call(
        pack_kernel,
        out_shape=pltpu.VMEM((Z, ROWS_IN, *tile), jnp.float32),
        in_specs=[SMEM] + [HBM] * 3,
        out_specs=VMEM,
        scratch_shapes=[
            pltpu.VMEM((Z * 2, SUB * LANES), jnp.float32),
            pltpu.VMEM((Z * 2, SUB * LANES), jnp.float32),
            pltpu.VMEM(tile, jnp.float32),
            pltpu.SemaphoreType.DMA((3,)),
        ],
        compiler_params=pltpu.CompilerParams(vmem_limit_bytes=60 * 1024 * 1024),
    )(scalar, out_grad, conv_input, filter_taps.reshape(tile))
    zone, core = lax.axis_index("z"), lax.axis_index("c")

    def toward(i, crossed):
        shift = jnp.where(core == crossed, SHIFTS[0][i], SHIFTS[1][i])
        return lax.dynamic_index_in_dim(packed, (zone + shift) & (Z - 1), 0, keepdims=False)

    given = swap_core(jnp.stack([toward(i, 1) for i in range(Z // 2)]))

    def exchange_z(messages, shifts):
        even = shifts[0][:KEPT] + (UNUSED,)
        moved = [shift_z(m, *by) for m, *by in zip(messages, even, shifts[1])]
        moved[KEPT] = jnp.where(core == 0, messages[KEPT], moved[KEPT])
        return moved

    steps = exchange_z([jnp.stack([toward(i, 0), given[i]]) for i in range(Z // 2)], SHIFTS)

    def z_forward(half):
        return pl.pallas_call(
            functools.partial(z_forward_kernel, half),
            out_shape=f32(X, C, ROWS_IN, 2, *tile),
            in_specs=[SMEM, SMEM] + [VMEM] * 4,
            out_specs=VMEM,
            compiler_params=PARAMS,
        )(scalar, zone.reshape(1), *steps)

    sent = z_forward(1)
    first = swap_core(sent[0])
    crossed = swap_core(sent[1:])
    kept = z_forward(0)
    chunks = [kept[0] + first] + [kept[i] + crossed[i - 1] for i in range(1, X)]
    place, chunks[X - 1] = lax.optimization_barrier((place, chunks[X - 1]))
    matrix, back = left_tables(ORDER_IN), np.swapaxes(left_tables(ORDER_OUT), 1, 2)
    left = mine(np.stack(numpy_split(matrix) + numpy_split(back), axis=1))
    twiddle = mine(twiddle_tables())
    chunks = [shift_x(chunk, s) if s else chunk for chunk, s in zip(chunks, ORDER_IN)]
    chunks = pl.pallas_call(
        spectral_kernel,
        out_shape=[f32(C, ROWS_OUT, 2, *tile)] * X,
        in_specs=[VMEM] * 7,
        out_specs=[VMEM] * X,
        compiler_params=PARAMS,
    )(*chunks, left, twiddle, right)
    chunks = [shift_x(chunk, -s) if s else chunk for chunk, s in zip(chunks, ORDER_OUT)]
    near = jnp.stack([chunk[0] for chunk in chunks])
    far = jnp.stack([chunk[1] for chunk in chunks])

    def z_return(half):
        return pl.pallas_call(
            functools.partial(z_return_kernel, half),
            out_shape=f32(Z // 2, C, ROWS_OUT, *tile),
            in_specs=[SMEM] * 2 + [VMEM] * 2,
            out_specs=VMEM,
            compiler_params=PARAMS,
        )(scalar, zone.reshape(1), near, far)

    crossed = swap_core(z_return(1))
    kept = z_return(0)
    steps = exchange_z([kept[i] + crossed[i] for i in range(Z // 2)], SHIFTS_BACK)
    others = swap_core(jnp.stack([step[1] for step in steps]))
    filter_grad = pl.pallas_call(
        filter_sum_kernel,
        out_shape=f32(*tile),
        in_specs=[VMEM] * 5,
        out_specs=VMEM,
        compiler_params=PARAMS,
    )(*steps, others)
    input_grad = pl.pallas_call(
        finish_kernel,
        out_shape=f32(Z, 2, *tile),
        in_specs=[SMEM] * 3 + [VMEM] * 6,
        out_specs=VMEM,
        compiler_params=PARAMS,
    )(scalar, zone.reshape(1), skip_gain, packed, *steps, others)
    across = pair_y(filter_grad, lambda i: i ^ 2)
    far = pair_y(filter_grad, lambda i: Y - 1 - i)
    near = pair_y(filter_grad, lambda i: i ^ 1)
    filter_grad = (filter_grad + near) + (far + across)
    return (input_grad.reshape(out_grad.shape), filter_grad.reshape(filter_taps.shape))


def solution(mesh):
    fine = Mesh(mesh.devices.reshape(Y, Z, X, C), ("y", "z", "x", "c"))
    return jax.shard_map(
        per_device,
        mesh=fine,
        in_specs=(P("y", None, ("z", "x", "c")), P("y", None, ("z", "x", "c")), P(("z", "x", "c")), P()),
        out_specs=(P("y", None, ("z", "x", "c")), P(("z", "x", "c"))),
        check_vma=False,
    )
```

```python
import functools
import math

import jax
import jax.numpy as jnp
import ml_dtypes
import numpy as np
from jax import lax
from jax.experimental import pallas as pl
from jax.experimental.pallas import tpu as pltpu
from jax.sharding import Mesh, PartitionSpec as P

Y, Z, X, C = 4, 8, 4, 2
ROWS_IN, ROWS_OUT = 5, 3
SHIFTS, SHIFTS_BACK = ((3, 1, 6, 0), (5, 7, 2, 4)), ((1, 6, 3, 0), (7, 2, 5, 4))
KEPT, UNUSED = 3, 7
ORDER_IN, ORDER_OUT = (2, 0, 1, 3), (0, 2, 1, 3)
SUB, LANES = 16, 128
POINTS = 128
SCALE = 1.0 / 131072.0


def class_of(x, c):
    return 2 * x + c


def came_from(zone, core, shifts):
    shift = jnp.where(core == 0, *shifts)
    return (zone - shift) & (Z - 1)


def turn(source, multiple):
    real, imag = jnp.float32(1.0), jnp.float32(0.0)
    for z in range(1, Z):
        angle = math.pi * multiple * z / 16.0
        real = jnp.where(source == z, jnp.float32(math.cos(angle)), real)
        imag = jnp.where(source == z, jnp.float32(-math.sin(angle)), imag)
    return real, imag


def slot_of(x, place, order):
    shift = (x - place // 2) & (X - 1)
    slot = jnp.int32(order.index(0))
    for other in range(1, X):
        slot = jnp.where(shift == other, order.index(other), slot)
    return slot


def numpy_split(table):
    table = table.astype(np.float32)
    high = table.astype(ml_dtypes.bfloat16)
    low = (table - high.astype(np.float32)).astype(ml_dtypes.bfloat16)
    return high, low


def left_tables(order):
    out = np.zeros((X * C, 2, POINTS, X, C, 2, SUB))
    alpha = np.arange(POINTS)[:, None]
    for x in range(X):
        for c in range(C):
            k = class_of(x, c) + 0.5
            for slot, shift in enumerate(order):
                for other in range(C):
                    p = class_of((x - shift) % X, c ^ other)
                    a = p * SUB + np.arange(SUB)[None, :]
                    angle = -2.0 * np.pi * ((a * alpha % POINTS) / POINTS + a * k / 2048.0)
                    at = out[class_of(x, c), :, :, slot, other]
                    at[0, :, 0], at[0, :, 1] = np.cos(angle), -np.sin(angle)
                    at[1, :, 0], at[1, :, 1] = np.sin(angle), np.cos(angle)
    return out.reshape(X * C, 2 * POINTS, 2 * POINTS)


def twiddle_tables():
    out = np.zeros((X * C, 2, POINTS, LANES))
    alpha, b = np.arange(POINTS)[:, None], np.arange(LANES)[None, :]
    for p in range(X * C):
        angle = -2.0 * np.pi * b * (alpha + (p + 0.5) / 16.0) / 16384.0
        out[p, 0], out[p, 1] = np.cos(angle), np.sin(angle)
    return out.astype(np.float32)


def right_table():
    b = np.arange(LANES)
    angle = -2.0 * np.pi * (b[:, None] * b[None, :] % LANES) / LANES
    cosine, sine = np.cos(angle), np.sin(angle)
    return np.block([[cosine, sine], [-sine, cosine]])


def pack_kernel(place_ref, grad_hbm, input_hbm, filter_hbm, out_ref, grad_ref, input_ref, filter_ref, sems):
    pairs = ((grad_hbm.at[0], grad_ref), (input_hbm.at[0], input_ref), (filter_hbm, filter_ref))
    copies = [pltpu.make_async_copy(*pair, sems.at[i]) for i, pair in enumerate(pairs)]
    for copy in copies:
        copy.start()
    for first, ref in ((0, grad_ref), (2, input_ref)):
        copies[first // 2].wait()
        values = ref[...].reshape(Z * 2, SUB, LANES)
        for z in range(Z):
            for row in range(2):
                out_ref[z, first + row] = values[2 * z + row]
    copies[2].wait()
    for z in range(Z):
        out_ref[z, 4] = filter_ref[...]


def z_forward_kernel(half, place_ref, zone_ref, m0, m1, m2, m3, out_ref):
    place, steps = place_ref[0], (m0, m1, m2, m3)
    core = place & 1
    parity = core ^ half
    weights, turns = [], []
    for i in range(len(steps)):
        source = came_from(zone_ref[0], core, (SHIFTS[0][i], SHIFTS[1][i]))
        starts = [turn(source, multiple) for multiple in (1, 3)]
        weights.append([
            jnp.full((SUB, LANES), jnp.where(parity == 0, low, high)) for low, high in zip(*starts)
        ])
        turns.append([jnp.full((SUB, LANES), part) for part in turn(source, 4)])
    for x in range(X):
        slot = slot_of(x, place, ORDER_IN)
        for part in range(2):
            for source in range(C):
                total = weights[0][part] * m0[source]
                for weight, ref in zip(weights[1:], steps[1:]):
                    total = total + weight[part] * ref[source]
                out_ref[slot, source ^ half, :, part] = total
        weights = [
            [real * re - imag * im, real * im + imag * re]
            for (real, imag), (re, im) in zip(weights, turns)
        ]


def z_return_kernel(half, place_ref, zone_ref, near_ref, far_ref, out_ref):
    place = place_ref[0]
    core = place & 1
    slots = [slot_of(x, place, ORDER_OUT) for x in range(X)]
    for i in range(Z // 2):
        shift = jnp.where(core == half, SHIFTS_BACK[0][i], SHIFTS_BACK[1][i])
        target = (zone_ref[0] + shift) & (Z - 1)
        starts = [turn(target, multiple) for multiple in (1, 3)]
        weight = [
            jnp.full((SUB, LANES), jnp.where(core == 0, low, high) * SCALE)
            for low, high in zip(*starts)
        ]
        re, im = [jnp.full((SUB, LANES), part) for part in turn(target, 4)]
        totals = [None, None]
        for x in range(X):
            for part in range(2):
                for block, ref in enumerate((near_ref, far_ref)):
                    term = weight[part] * ref[slots[x], :, part]
                    totals[block] = term if totals[block] is None else totals[block] + term
            real, imag = weight
            weight = [real * re - imag * im, real * im + imag * re]
        for block in range(2):
            out_ref[i, block ^ half] = totals[block]


def filter_sum_kernel(r0, r1, r2, r3, own_ref, other_ref):
    for block, out_ref in enumerate((own_ref, other_ref)):
        out_ref[...] = (r0[block, 2] + r1[block, 2]) + (r2[block, 2] + r3[block, 2])


def finish_kernel(place_ref, zone_ref, skip_ref, packed_ref, r0, r1, r2, r3, other_ref, out_ref):
    core = place_ref[0] & 1
    for half in range(2):
        for i, ref in enumerate((r0, r1, r2, r3)):
            shifts = (SHIFTS_BACK[0][i], SHIFTS_BACK[1][i])
            source = came_from(zone_ref[0], core ^ half, shifts)
            for row in range(2):
                value = other_ref[i, row] if half else ref[0, row]
                out_ref[source, row] = value + skip_ref[2 * source + row] * packed_ref[source, row]


def split(value):
    high = value.astype(jnp.bfloat16)
    return high, (value - high.astype(jnp.float32)).astype(jnp.bfloat16)


def product(left, right):
    (left_high, left_low), (right_high, right_low) = left, right
    dot = functools.partial(jnp.dot, preferred_element_type=jnp.float32)
    return dot(left_high, right_high) + (dot(left_high, right_low) + dot(left_low, right_high))


def spectral_kernel(
    x0, x1, x2, x3, left, tw, right, o0, o1, o2, o3
):
    chunks, outs = (x0, x1, x2, x3), (o0, o1, o2, o3)
    wh, wl, wth, wtl = (left[i] for i in range(4))
    bh, bl, bth, btl = (right[i] for i in range(4))
    pieces = [(s, c, part) for s in range(X) for c in range(C) for part in range(2)]
    cosine, sine = tw[0], tw[1]

    def forward(*picked):
        columns = [
            jnp.concatenate([chunks[s][c, row, part] for s, c, part in pieces], axis=0)
            for row in picked
        ]
        value = product((wh, wl), split(jnp.concatenate(columns, axis=1)))
        rows = []
        for i in range(len(picked)):
            lanes = slice(i * LANES, (i + 1) * LANES)
            real, imag = value[:POINTS, lanes], value[POINTS:, lanes]
            rows.append(
                jnp.concatenate([real * cosine - imag * sine, real * sine + imag * cosine], axis=1)
            )
        value = product(split(jnp.concatenate(rows, axis=0)), (bh, bl))
        spans = [slice(i * POINTS, (i + 1) * POINTS) for i in range(len(picked))]
        return [(value[span, :LANES], value[span, LANES:]) for span in spans]

    def inverse(spectra, picked):
        rows = jnp.concatenate([jnp.concatenate(pair, axis=1) for pair in spectra], axis=0)
        value = product(split(rows), (bth, btl))
        columns = []
        for i in range(len(picked)):
            span = slice(i * POINTS, (i + 1) * POINTS)
            vr, vi = value[span, :LANES], value[span, LANES:]
            columns.append(
                jnp.concatenate([vr * cosine + vi * sine, vi * cosine - vr * sine], axis=0)
            )
        value = product((wth, wtl), split(jnp.concatenate(columns, axis=1)))
        for index, (s, c, part) in enumerate(pieces):
            for i, row in enumerate(picked):
                outs[s][c, row, part] = value[
                    index * SUB : (index + 1) * SUB, i * LANES : (i + 1) * LANES
                ]

    ((fr, fi),) = forward(4)
    pairs = [forward(channel, 2 + channel) for channel in range(2)]
    inverse([(fr * gr + fi * gi, fr * gi - fi * gr) for (gr, gi), _ in pairs], (0, 1))
    dh_real, dh_imag = 0.0, 0.0
    for (gr, gi), (ur, ui) in pairs:
        dh_real = dh_real + (gr * ur + gi * ui)
        dh_imag = dh_imag + (gi * ur - gr * ui)
    inverse([(dh_real, dh_imag)], (2,))


VMEM = pl.BlockSpec(memory_space=pltpu.VMEM)
HBM = pl.BlockSpec(memory_space=pltpu.HBM)
SMEM = pl.BlockSpec(memory_space=pltpu.SMEM)
PARAMS = pltpu.CompilerParams(vmem_limit_bytes=32 * 1024 * 1024)


def f32(*shape):
    return jax.ShapeDtypeStruct(shape, jnp.float32)


def shift_x(value, shift):
    return lax.ppermute(value, "x", [(i, (i + shift) % X) for i in range(X)])


def shift_z(value, even, odd):
    pairs = [(C * z + c, C * ((z + by) % Z) + c) for c, by in enumerate((even, odd)) for z in range(Z)]
    return lax.ppermute(value, ("z", "c"), pairs)


def swap_core(value):
    return lax.ppermute(value, "c", [(0, 1), (1, 0)])


def pair_y(value, partner):
    return lax.ppermute(value, "y", [(i, partner(i)) for i in range(Y)])


def per_device(out_grad, conv_input, filter_taps, skip_gain):
    place = class_of(lax.axis_index("x"), lax.axis_index("c"))

    def mine(table):
        return lax.dynamic_index_in_dim(jnp.asarray(table), place, 0, keepdims=False)

    tile = (SUB, LANES)
    scalar = place.reshape(1)
    matrix = right_table()
    right = jnp.asarray(np.stack(numpy_split(matrix) + numpy_split(matrix.T)))

    packed = pl.pallas_call(
        pack_kernel,
        out_shape=pltpu.VMEM((Z, ROWS_IN, *tile), jnp.float32),
        in_specs=[SMEM] + [HBM] * 3,
        out_specs=VMEM,
        scratch_shapes=[
            pltpu.VMEM((Z * 2, SUB * LANES), jnp.float32),
            pltpu.VMEM((Z * 2, SUB * LANES), jnp.float32),
            pltpu.VMEM(tile, jnp.float32),
            pltpu.SemaphoreType.DMA((3,)),
        ],
        compiler_params=pltpu.CompilerParams(vmem_limit_bytes=60 * 1024 * 1024),
    )(scalar, out_grad, conv_input, filter_taps.reshape(tile))
    zone, core = lax.axis_index("z"), lax.axis_index("c")

    def toward(i, crossed):
        shift = jnp.where(core == crossed, SHIFTS[0][i], SHIFTS[1][i])
        return lax.dynamic_index_in_dim(packed, (zone + shift) & (Z - 1), 0, keepdims=False)

    given = swap_core(jnp.stack([toward(i, 1) for i in range(Z // 2)]))

    def exchange_z(messages, shifts):
        even = shifts[0][:KEPT] + (UNUSED,)
        moved = [shift_z(m, *by) for m, *by in zip(messages, even, shifts[1])]
        moved[KEPT] = jnp.where(core == 0, messages[KEPT], moved[KEPT])
        return moved

    steps = exchange_z([jnp.stack([toward(i, 0), given[i]]) for i in range(Z // 2)], SHIFTS)

    def z_forward(half):
        return pl.pallas_call(
            functools.partial(z_forward_kernel, half),
            out_shape=f32(X, C, ROWS_IN, 2, *tile),
            in_specs=[SMEM, SMEM] + [VMEM] * 4,
            out_specs=VMEM,
            compiler_params=PARAMS,
        )(scalar, zone.reshape(1), *steps)

    sent = z_forward(1)
    first = swap_core(sent[0])
    crossed = swap_core(sent[1:])
    kept = z_forward(0)
    chunks = [kept[0] + first] + [kept[i] + crossed[i - 1] for i in range(1, X)]
    place, chunks[X - 1] = lax.optimization_barrier((place, chunks[X - 1]))
    matrix, back = left_tables(ORDER_IN), np.swapaxes(left_tables(ORDER_OUT), 1, 2)
    left = mine(np.stack(numpy_split(matrix) + numpy_split(back), axis=1))
    twiddle = mine(twiddle_tables())
    chunks = [shift_x(chunk, s) if s else chunk for chunk, s in zip(chunks, ORDER_IN)]
    chunks = pl.pallas_call(
        spectral_kernel,
        out_shape=[f32(C, ROWS_OUT, 2, *tile)] * X,
        in_specs=[VMEM] * 7,
        out_specs=[VMEM] * X,
        compiler_params=PARAMS,
    )(*chunks, left, twiddle, right)
    chunks = [shift_x(chunk, -s) if s else chunk for chunk, s in zip(chunks, ORDER_OUT)]
    near = jnp.stack([chunk[0] for chunk in chunks])
    far = jnp.stack([chunk[1] for chunk in chunks])

    def z_return(half):
        return pl.pallas_call(
            functools.partial(z_return_kernel, half),
            out_shape=f32(Z // 2, C, ROWS_OUT, *tile),
            in_specs=[SMEM] * 2 + [VMEM] * 2,
            out_specs=VMEM,
            compiler_params=PARAMS,
        )(scalar, zone.reshape(1), near, far)

    crossed = swap_core(z_return(1))
    kept = z_return(0)
    steps = exchange_z([kept[i] + crossed[i] for i in range(Z // 2)], SHIFTS_BACK)
    filter_own, filter_other = pl.pallas_call(
        filter_sum_kernel,
        out_shape=[f32(*tile)] * 2,
        in_specs=[VMEM] * 4,
        out_specs=[VMEM] * 2,
        compiler_params=PARAMS,
    )(*steps)
    filter_grad = filter_own + swap_core(filter_other)
    others = swap_core(jnp.stack([step[1, :2] for step in steps]))
    input_grad = pl.pallas_call(
        finish_kernel,
        out_shape=f32(Z, 2, *tile),
        in_specs=[SMEM] * 3 + [VMEM] * 6,
        out_specs=VMEM,
        compiler_params=PARAMS,
    )(scalar, zone.reshape(1), skip_gain, packed, *steps, others)
    across = pair_y(filter_grad, lambda i: i ^ 2)
    far = pair_y(filter_grad, lambda i: Y - 1 - i)
    near = pair_y(filter_grad, lambda i: i ^ 1)
    input_grad = input_grad.reshape(out_grad.shape)
    filter_grad, input_grad = lax.optimization_barrier((filter_grad, input_grad))
    filter_grad = (filter_grad + near) + (far + across)
    return (input_grad, filter_grad.reshape(filter_taps.shape))


def solution(mesh):
    fine = Mesh(mesh.devices.reshape(Y, Z, X, C), ("y", "z", "x", "c"))
    return jax.shard_map(
        per_device,
        mesh=fine,
        in_specs=(P("y", None, ("z", "x", "c")), P("y", None, ("z", "x", "c")), P(("z", "x", "c")), P()),
        out_specs=(P("y", None, ("z", "x", "c")), P(("z", "x", "c"))),
        check_vma=False,
    )
```
